128 devices in a mesh: blk: 32 (over z, x, core), grp: 4 (over y).
Axes of the slice: x: 4, y: 4, z: 4, core: 2. Of those that a mesh axis runs over, the one named last changes fastest.
Arguments:
- image_emb: float32 [16384, 1152], P(('blk', 'grp')), may hold values from -0.18 to 0.18
- text_emb: float32 [16384, 1152], P(('blk', 'grp')), may hold values from -0.18 to 0.18
- logit_scale: float32 [1], replicated, may hold values from 6 to 12
- logit_bias: float32 [1], replicated, may hold values from -5 to -3
- pos_image: int32 [16384, 4], P(('blk', 'grp')), may hold values from 0 to 16383, as said below
- pos_count: int32 [16384], P(('blk', 'grp')), may hold values from 1 to 4, as said below
- image_row: int32 [16384], P(('blk', 'grp')), may hold values from 0 to 16383, as said below
Outputs:
- grad_image: float32 [16384, 1152], P(('blk', 'grp'))
- grad_text: float32 [16384, 1152], P(('blk', 'grp'))
The draws below stay inside these ranges and needn't reach their ends.
Inputs may be any that keep to these rules, and one draw needn't show every extreme that they name: `pos_image`: only the first pos_count entries of a row count; all 4 entries of a row are distinct ids of the caption's own group: a caption in rows g * 512 to (g + 1) * 512 - 1 names ids in that same range. `pos_count`: some caption has 4 positives and some has one. `image_row`: A permutation that maps the ids of each group of 512 onto the rows of the same group.
All inputs are finite; a program needn't handle non-finite values.
Results may differ from the reference program's by a relative error of at most 0.00014.
Values sent between devices are 32-bit elements; how exact they have to be, the bound alone decides.
A program may use at most 128 MiB of HBM per device.

```python
import jax
import jax.numpy as jnp
from jax import lax

D = 1152
ROWS = 128
P_SIZE = 4
GROUP = 512
COLUMN = 4096
B = 16384
N_BLK = 32
N_GRP = 4


def draw_pos_image(key, part):
    key = jax.random.fold_in(key, 11)
    scores = jax.random.randint(key, (B, GROUP), 0, 2 ** 20) * GROUP + jnp.arange(GROUP, dtype=jnp.int32)[None, :]
    order = jnp.argsort(scores, axis=1, stable=True)[:, :P_SIZE]
    base = jnp.arange(B, dtype=jnp.int32) // GROUP * GROUP
    return (base[:, None] + order).astype(jnp.int32)


def draw_pos_count(key, part):
    key = jax.random.fold_in(key, 12)
    first_key, second_key = jax.random.split(key)
    first = jax.random.randint(first_key, (B,), 1, P_SIZE + 1)
    second = jax.random.randint(second_key, (B,), 1, P_SIZE + 1)
    counts = jnp.minimum(first, second)
    counts = counts.at[0].set(P_SIZE).at[1].set(1)
    return counts.astype(jnp.int32)


def draw_image_row(key, part):
    key = jax.random.fold_in(key, 13)
    scores = jax.random.randint(key, (B // GROUP, GROUP), 0, 2 ** 20) * GROUP + jnp.arange(GROUP, dtype=jnp.int32)[None, :]
    order = jnp.argsort(scores, axis=1, stable=True)
    base = jnp.arange(B // GROUP, dtype=jnp.int32)[:, None] * GROUP
    return (base + order).reshape(B).astype(jnp.int32)


def block_scale(stream_key, dims, cuts, low, high):
    def one(axis_at, blocks):
        heights = jax.random.uniform(jax.random.fold_in(jax.random.fold_in(stream_key, 6), axis_at), (blocks,), jnp.float32, low / len(cuts), high / len(cuts))
        return jnp.repeat(jnp.exp(heights), dims[axis_at] // blocks).reshape((-1,) + (1,) * (len(dims) - axis_at - 1))

    level = one(*cuts[0])
    for cut in cuts[1:]:
        level = level * one(*cut)
    return level


def normal_values(key, extent, width, limit, cuts=(), kind=jnp.bfloat16):
    result = jax.random.normal(key, extent, jnp.float32) * width
    if len(cuts) > 0:
        result = block_scale(key, extent, cuts, -0.22, 0.18) * result
    return jnp.clip(result, min=-limit, max=limit).astype(kind)


def setup_inputs(seed: int = 0) -> dict:
    streams_of = jax.random.split(jax.random.key(seed), 8)
    return {
        "image_emb": normal_values(streams_of[0], (B, D), 0.03, 0.18, ((0, 128),), jnp.float32),
        "text_emb": normal_values(streams_of[1], (B, D), 0.03, 0.18, ((0, 128),), jnp.float32),
        "logit_scale": jnp.clip(jax.random.uniform(streams_of[2], (1,), jnp.float32, 6.0, 12.0), 6.0, 12.0),
        "logit_bias": jnp.clip(jax.random.uniform(streams_of[3], (1,), jnp.float32, -5.0, -3.0), -5.0, -3.0),
        "pos_image": draw_pos_image(jax.random.fold_in(streams_of[7], 71), 0),
        "pos_count": draw_pos_count(jax.random.fold_in(streams_of[7], 71), 0),
        "image_row": draw_image_row(jax.random.fold_in(streams_of[7], 71), 0),
    }


def normalize(values):
    norms = jnp.sqrt(lax.optimization_barrier(jnp.sum(values * values, axis=1, keepdims=True)) + 1e-06)
    return (values / norms, norms)

def product(left, right):
    return jnp.dot(left, right, precision=lax.Precision.HIGHEST, preferred_element_type=jnp.float32)

def unproject(grad_unit, unit, norms):
    return (grad_unit - unit * lax.optimization_barrier(jnp.sum(unit * grad_unit, axis=1, keepdims=True))) / norms

def to_columns(values):
    return values.reshape(N_BLK, N_GRP, ROWS, D).transpose(1, 0, 2, 3).reshape(N_GRP, COLUMN, D)

def from_columns(values):
    return values.reshape(N_GRP, N_BLK, ROWS, D).transpose(1, 0, 2, 3).reshape(B, D)

def reference(image_emb, text_emb, logit_scale, logit_bias, pos_image, pos_count, image_row):
    unit_img, img_norm = normalize(image_emb)
    unit_txt, txt_norm = normalize(text_emb)
    temper = logit_scale[0]
    offset = logit_bias[0]

    def one_column(pair):
        images, texts = pair
        sigmas = jax.nn.sigmoid(temper * product(images, texts.T) + offset)
        return (temper * product(sigmas, texts), temper * product(sigmas.T, images))
    col_img, col_txt = lax.map(one_column, (to_columns(unit_img), to_columns(unit_txt)))
    grad_img = from_columns(col_img)
    grad_txt = from_columns(col_txt)
    target = jnp.take(image_row, pos_image, axis=0).astype(jnp.int32)
    valid = (jnp.arange(P_SIZE, dtype=jnp.int32)[None, :] < pos_count[:, None]).astype(grad_img.dtype)
    caption_column = jnp.arange(B, dtype=jnp.int32) // ROWS % N_GRP
    for slot in range(P_SIZE):
        rows_now = target[:, slot]
        img_rows = jnp.take(unit_img, rows_now, axis=0)
        pair_logit = temper * lax.optimization_barrier(jnp.sum(img_rows * unit_txt, axis=1)) + offset
        same = rows_now // ROWS % N_GRP == caption_column
        coef = valid[:, slot] * jnp.where(same, -1.0, jax.nn.sigmoid(pair_logit) - 1.0)
        grad_img = grad_img.at[rows_now].add(temper * coef[:, None] * unit_txt)
        grad_txt = grad_txt + temper * coef[:, None] * img_rows
    return (unproject(grad_img, unit_img, img_norm), unproject(grad_txt, unit_txt, txt_norm))
```

```python
import functools

import jax
import jax.numpy as jnp
from jax import lax
from jax.experimental import pallas as pl
from jax.experimental.pallas import tpu as pltpu
from jax.sharding import PartitionSpec as P

ROWS = 128
HALF = 64
PIECE = 32
D = 1152
COLS = ((0, 256), (256, 256), (512, 256), (768, 256), (1024, 128))
N_COPIES = 80
F32 = jnp.float32
BF16 = jnp.bfloat16


def rows_at(start, count):
    return pl.ds(start, count)


def split(values):
    high = values.astype(BF16)
    return high, (values - high.astype(F32)).astype(BF16)


def dot_nn(a, b):
    return lax.dot_general(a, b, (((1,), (0,)), ((), ())), preferred_element_type=F32)


def dot_nt(a, b):
    return lax.dot_general(a, b, (((1,), (1,)), ((), ())), preferred_element_type=F32)


def kernel(
    scale_ref, bias_ref, img_ref, txt_ref, pos_ref, cnt_ref, row_ref,
    gimg_ref, gtxt_ref,
    img, txt, img_hi, img_lo, txt_hi, txt_lo, sig, g_img, g_txt,
    y_txt, y_img, yt_hi, yt_lo, yi_hi, yi_lo,
    x_in, z_in, c_in, meta, mark_a, mark_b, norm_img, norm_txt, send_sem, recv_sem,
):
    blk, grp = lax.axis_index("blk"), lax.axis_index("grp")
    core = lax.rem(blk, 2)
    x = lax.rem(lax.div(blk, 2), 4)
    z = lax.div(blk, 8)

    def place(dz, dx, dg):
        zz, xx, gg = lax.rem(z + dz, 4), lax.rem(x + dx, 4), lax.rem(grp + dg, 4)
        return ((zz * 4 + xx) * 2 + core, gg)

    x_dev = (place(0, 1, 0), place(0, 3, 0))
    z_dev = (place(1, 0, 0), place(3, 0, 0))
    y_dev = (place(0, 0, 1), place(0, 0, 3))
    y_far = place(0, 0, 2)
    peer = ((z * 4 + x) * 2 + 1 - core, grp)
    partners = x_dev + z_dev + y_dev + (y_far, peer)

    barrier = pltpu.get_barrier_semaphore()
    for other in partners:
        pl.semaphore_signal(barrier, inc=1, device_id=other, device_id_type=pl.DeviceIdType.MESH)

    temper = scale_ref[0]
    offset = bias_ref[0]

    for source, unit, norm in ((img_ref, img, norm_img), (txt_ref, txt, norm_txt)):
        values = source[...]
        length = jnp.sqrt(jnp.sum(values * values, axis=1, keepdims=True) + 1e-06)
        norm[...] = length
        unit[0:ROWS, :] = values / length
    meta[0, 0:4, :] = pos_ref[...]
    meta[0, 4:5, :] = cnt_ref[...]
    meta[0, 5:6, :] = row_ref[...]
    meta[0, 6:8, :] = jnp.zeros((2, ROWS), jnp.int32)

    pl.semaphore_wait(barrier, len(partners))

    copies = {}

    def push(name, source, target, device):
        at = len(copies)
        copy = pltpu.make_async_remote_copy(
            src_ref=source, dst_ref=target, send_sem=send_sem.at[at], recv_sem=recv_sem.at[at],
            device_id=device, device_id_type=pl.DeviceIdType.MESH,
        )
        copy.start()
        copies[name] = copy

    def arrived(name):
        copies[name].wait_recv()

    rings = {"x": (img, 2 * ROWS, x_dev), "z": (txt, ROWS, z_dev)}

    def gather(axis, step, side, part):
        buffer, stride, devices = rings[axis]
        first = {1: side * HALF, 2: stride + side * HALF, 3: (1 - side) * HALF}[step]
        push(
            (axis, step, side, part),
            buffer.at[rows_at(first + part * PIECE, PIECE)],
            buffer.at[rows_at(stride * step + side * HALF + part * PIECE, PIECE)],
            devices[side],
        )

    y_rings = {"yt": (txt, y_txt), "yi": (img, y_img)}

    def gather_y(axis, step, side):
        own, others = y_rings[axis]
        half = side if step != 2 else 1 - side
        if step == 3:
            source = others.at[rows_at(side * ROWS + side * HALF, HALF)]
            target = others.at[rows_at(2 * ROWS + side * HALF, HALF)]
        else:
            source = own.at[rows_at(half * HALF, HALF)]
            target = others.at[rows_at(side * ROWS + half * HALF, HALF)]
        push((axis, step, side), source, target, y_dev[side])

    def across(step):
        first = 2 * ROWS * step
        push(("c", step), img.at[rows_at(first, ROWS)], img.at[rows_at(first + ROWS, ROWS)], peer)

    def split_rows(source, high, low, first, count):
        for at in range(first, first + count, HALF):
            high[at:at + HALF, :], low[at:at + HALF, :] = split(source[at:at + HALF, :])

    def sigmoids(row, rows, col, cols):
        def one(at, count):
            a_hi, a_lo = img_hi[rows_at(at, count), :], img_lo[rows_at(at, count), :]
            b_hi, b_lo = txt_hi[col:col + cols, :], txt_lo[col:col + cols, :]
            dots = dot_nt(a_hi, b_hi) + (dot_nt(a_hi, b_lo) + dot_nt(a_lo, b_hi))
            sig[rows_at(at, count), col:col + cols] = jax.nn.sigmoid(temper * dots + offset)

        if rows <= 256:
            one(row, rows)
        else:
            def turn(i, carry):
                one(pl.multiple_of(row + i * 256, 256), 256)
                return carry

            lax.fori_loop(0, rows // 256, turn, 0)

    def times(left, high, low, store):
        l_hi, l_lo = split(left)
        for at, count in COLS:
            cs = slice(at, at + count)
            store(cs, dot_nn(l_hi, high[:, cs]) + (dot_nn(l_hi, low[:, cs]) + dot_nn(l_lo, high[:, cs])))

    def image_grads(first):
        def store(cs, value):
            g_img[first:first + ROWS, cs] = value

        times(sig[first:first + ROWS, :], txt_hi, txt_lo, store)

    def text_grads(first):
        def store(cs, value):
            g_txt[first:first + ROWS, cs] = value

        times(sig[:, first:first + ROWS].T, img_hi, img_lo, store)

    for slot, device in ((1, y_dev[0]), (2, y_dev[1]), (3, y_far)):
        push(("m", slot), meta.at[0], meta.at[slot], device)
    for part in (0, 1):
        for axis in ("x", "z"):
            for side in (0, 1):
                gather(axis, 1, side, part)
    across(0)
    for step in (1, 2):
        for side in (0, 1):
            gather_y("yt", step, side)

    split_rows(img, img_hi, img_lo, 0, ROWS)
    split_rows(txt, txt_hi, txt_lo, 0, ROWS)
    arrived(("c", 0))
    split_rows(img, img_hi, img_lo, ROWS, ROWS)
    sigmoids(0, 256, 0, ROWS)

    for slot in (1, 2, 3):
        arrived(("m", slot))
    group_base = blk * (4 * ROWS)
    places = [lax.rem(grp + shift, 4) * ROWS + group_base for shift in (0, 3, 1, 2)]
    tall = lax.broadcasted_iota(jnp.int32, (ROWS, ROWS), 0)

    def named(slot):
        tiles = []
        for ids in range(4):
            hit = None
            for k in range(4):
                listed = jnp.where(meta[slot, 4:5, :] > k, meta[slot, k:k + 1, :], -1)
                same = listed == tall + places[ids]
                hit = same if hit is None else hit | same
            tiles.append(jnp.where(hit, 1.0, 0.0).astype(BF16))
        return jnp.concatenate(tiles, axis=0)

    def held(slot):
        tiles = [
            jnp.where(meta[ids, 5:6, :] == tall + places[slot], 1.0, 0.0).astype(BF16)
            for ids in range(4)
        ]
        return jnp.concatenate(tiles, axis=1)

    for part in (0, 1):
        for axis in ("x", "z"):
            for side in (0, 1):
                arrived((axis, 1, side, part))
                gather(axis, 2, side, part)
    across(1)
    for part in (0, 1):
        for axis in ("x", "z"):
            for side in (0, 1):
                gather(axis, 3, side, part)
    for side in (0, 1):
        arrived(("yt", 1, side))
        gather_y("yt", 3, side)
    for step in (1, 2):
        for side in (0, 1):
            gather_y("yi", step, side)

    split_rows(txt, txt_hi, txt_lo, ROWS, ROWS)
    split_rows(img, img_hi, img_lo, 256, ROWS)
    arrived(("c", 1))
    split_rows(img, img_hi, img_lo, 256 + ROWS, ROWS)
    sigmoids(256, 256, 0, 256)
    sigmoids(0, 256, ROWS, ROWS)

    own_ids, own_held = named(0), held(0)
    mark_a[:, 0:ROWS] = dot_nn(own_held, own_ids)
    for slot in (1, 2, 3):
        mark_a[:, slot * ROWS:(slot + 1) * ROWS] = dot_nn(own_held, named(slot))
        mark_b[(slot - 1) * ROWS:slot * ROWS, :] = dot_nn(held(slot), own_ids)

    for part in (0, 1):
        for axis in ("x", "z"):
            for side in (0, 1):
                arrived((axis, 2, side, part))
    across(2)
    split_rows(txt, txt_hi, txt_lo, 2 * ROWS, ROWS)
    split_rows(img, img_hi, img_lo, 512, ROWS)
    arrived(("c", 2))
    split_rows(img, img_hi, img_lo, 512 + ROWS, ROWS)
    sigmoids(512, 256, 0, 3 * ROWS)
    sigmoids(0, 512, 2 * ROWS, ROWS)

    for part in (0, 1):
        for side in (0, 1):
            arrived(("x", 3, side, part))
    across(3)
    for part in (0, 1):
        for side in (0, 1):
            arrived(("z", 3, side, part))
    split_rows(txt, txt_hi, txt_lo, 3 * ROWS, ROWS)
    sigmoids(512, 256, 3 * ROWS, ROWS)

    def share(step):
        first = 2 * ROWS * step
        push(("r", step), g_img.at[rows_at(first + ROWS, ROWS)], c_in.at[step], peer)

    def joined(step):
        first = 2 * ROWS * step
        arrived(("r", step))
        g_img[first:first + ROWS, :] += c_in[step]

    scatters = {"x": (g_img, 2 * ROWS, x_dev, x_in), "z": (g_txt, ROWS, z_dev, z_in)}

    def scatter(axis, turn):
        buffer, stride, devices, inbox = scatters[axis]
        for side in (0, 1):
            first = (2 * stride + side * HALF, stride + (1 - side) * HALF, 3 * stride + (1 - side) * HALF)[turn]
            if turn == 2:
                arrived((axis, "s", 0, side))
                buffer[first:first + HALF, :] += inbox[side, 0]
            push((axis, "s", turn, side), buffer.at[rows_at(first, HALF)], inbox.at[side, turn], devices[side])

    image_grads(512 + ROWS)
    share(2)
    image_grads(512)
    split_rows(img, img_hi, img_lo, 768, ROWS)
    arrived(("c", 3))
    split_rows(img, img_hi, img_lo, 768 + ROWS, ROWS)
    sigmoids(768, 256, 2 * ROWS, ROWS)
    joined(2)
    scatter("x", 0)
    text_grads(2 * ROWS)
    scatter("z", 0)

    sigmoids(0, 512, 3 * ROWS, ROWS)
    image_grads(256 + ROWS)
    share(1)
    image_grads(256)
    sigmoids(768, 256, 0, 2 * ROWS)
    joined(1)
    scatter("x", 1)
    text_grads(ROWS)
    scatter("z", 1)

    sigmoids(768, 256, 3 * ROWS, ROWS)
    image_grads(768 + ROWS)
    share(3)
    image_grads(768)
    joined(3)
    scatter("x", 2)
    text_grads(3 * ROWS)
    scatter("z", 2)

    for side in (0, 1):
        arrived(("yi", 1, side))
        gather_y("yi", 3, side)

    image_grads(ROWS)
    share(0)
    sig[0:ROWS, 0:ROWS] -= mark_a[:, 0:ROWS]
    image_grads(0)
    text_grads(0)

    for side in (0, 1):
        arrived(("yt", 2, side))
        arrived(("yt", 3, side))
    split_rows(y_txt, yt_hi, yt_lo, 0, 3 * ROWS)
    own = rows_at(0, ROWS)
    dots = dot_nt(img_hi[own, :], yt_hi[...]) + (dot_nt(img_hi[own, :], yt_lo[...]) + dot_nt(img_lo[own, :], yt_hi[...]))
    coef = mark_a[:, ROWS:4 * ROWS] * (jax.nn.sigmoid(temper * dots + offset) - 1.0)

    def add_img(cs, value):
        g_img[0:ROWS, cs] += value

    times(coef, yt_hi, yt_lo, add_img)
    joined(0)

    for side in (0, 1):
        arrived(("yi", 2, side))
        arrived(("yi", 3, side))
    split_rows(y_img, yi_hi, yi_lo, 0, 3 * ROWS)
    dots = dot_nt(yi_hi[...], txt_hi[own, :]) + (dot_nt(yi_hi[...], txt_lo[own, :]) + dot_nt(yi_lo[...], txt_hi[own, :]))
    coef = mark_b[...] * (jax.nn.sigmoid(temper * dots + offset) - 1.0)

    def add_txt(cs, value):
        g_txt[0:ROWS, cs] += value

    times(coef.T, yi_hi, yi_lo, add_txt)

    for axis, sums, inbox, unit, norm, out in (
        ("x", g_img, x_in, img, norm_img, gimg_ref),
        ("z", g_txt, z_in, txt, norm_txt, gtxt_ref),
    ):
        for turn in (1, 2):
            for side in (0, 1):
                arrived((axis, "s", turn, side))
        for half in (0, 1):
            at = slice(half * HALF, (half + 1) * HALF)
            grad = temper * (sums[at, :] + inbox[1 - half, 1] + inbox[half, 2])
            units = unit[at, :]
            along = jnp.sum(units * grad, axis=1, keepdims=True)
            out[at, :] = (grad - units * along) / norm[at, :]

    for copy in copies.values():
        copy.wait_send()


def body(image_emb, text_emb, logit_scale, logit_bias, pos_image, pos_count, image_row):
    smem = pl.BlockSpec(memory_space=pltpu.SMEM)
    vmem = pl.BlockSpec(memory_space=pltpu.VMEM)
    rows = jax.ShapeDtypeStruct((ROWS, D), F32)
    return pl.pallas_call(
        kernel,
        out_shape=(rows, rows),
        in_specs=[smem, smem, vmem, vmem, vmem, vmem, vmem],
        out_specs=(vmem, vmem),
        scratch_shapes=[
            pltpu.VMEM((8 * ROWS, D), F32),
            pltpu.VMEM((4 * ROWS, D), F32),
            pltpu.VMEM((8 * ROWS, D), BF16),
            pltpu.VMEM((8 * ROWS, D), BF16),
            pltpu.VMEM((4 * ROWS, D), BF16),
            pltpu.VMEM((4 * ROWS, D), BF16),
            pltpu.VMEM((8 * ROWS, 4 * ROWS), F32),
            pltpu.VMEM((8 * ROWS, D), F32),
            pltpu.VMEM((4 * ROWS, D), F32),
            pltpu.VMEM((3 * ROWS, D), F32),
            pltpu.VMEM((3 * ROWS, D), F32),
            pltpu.VMEM((3 * ROWS, D), BF16),
            pltpu.VMEM((3 * ROWS, D), BF16),
            pltpu.VMEM((3 * ROWS, D), BF16),
            pltpu.VMEM((3 * ROWS, D), BF16),
            pltpu.VMEM((2, 3, HALF, D), F32),
            pltpu.VMEM((2, 3, HALF, D), F32),
            pltpu.VMEM((4, ROWS, D), F32),
            pltpu.VMEM((4, 8, ROWS), jnp.int32),
            pltpu.VMEM((ROWS, 4 * ROWS), F32),
            pltpu.VMEM((3 * ROWS, ROWS), F32),
            pltpu.VMEM((ROWS, 1), F32),
            pltpu.VMEM((ROWS, 1), F32),
            pltpu.SemaphoreType.DMA((N_COPIES,)),
            pltpu.SemaphoreType.DMA((N_COPIES,)),
        ],
        compiler_params=pltpu.CompilerParams(
            collective_id=0, has_side_effects=True, vmem_limit_bytes=56 * 2**20
        ),
        name="align_step",
    )(
        logit_scale, logit_bias, image_emb, text_emb,
        pos_image.T, pos_count.reshape(1, ROWS), image_row.reshape(1, ROWS),
    )


def solution(mesh):
    return jax.shard_map(
        body,
        mesh=mesh,
        in_specs=(
            P(("blk", "grp"), None),
            P(("blk", "grp"), None),
            P(),
            P(),
            P(("blk", "grp"), None),
            P(("blk", "grp")),
            P(("blk", "grp")),
        ),
        out_specs=(P(("blk", "grp"), None), P(("blk", "grp"), None)),
        check_vma=False,
    )
```

```python
import functools

import jax
import jax.numpy as jnp
from jax import lax
from jax.experimental import pallas as pl
from jax.experimental.pallas import tpu as pltpu
from jax.sharding import PartitionSpec as P

ROWS = 128
HALF = 64
PIECE = 32
D = 1152
COLS = ((0, 256), (256, 256), (512, 256), (768, 256), (1024, 128))
N_COPIES = 80
F32 = jnp.float32
BF16 = jnp.bfloat16


def rows_at(start, count):
    return pl.ds(start, count)


def split(values):
    high = values.astype(BF16)
    return high, (values - high.astype(F32)).astype(BF16)


def dot_nn(a, b):
    return lax.dot_general(a, b, (((1,), (0,)), ((), ())), preferred_element_type=F32)


def dot_nt(a, b):
    return lax.dot_general(a, b, (((1,), (1,)), ((), ())), preferred_element_type=F32)


def kernel(
    scale_ref, bias_ref, img_hbm, txt_hbm, pos_hbm, cnt_hbm, row_hbm,
    gimg_ref, gtxt_ref,
    img_ref, txt_ref, pos_ref, cnt_ref, row_ref, load_sem,
    img, txt, img_hi, img_lo, txt_hi, txt_lo, sig, g_img, g_txt,
    y_txt, y_img, yt_hi, yt_lo, yi_hi, yi_lo,
    x_in, z_in, c_in, meta, mark_a, mark_b, norm_img, norm_txt, send_sem, recv_sem,
):
    blk, grp = lax.axis_index("blk"), lax.axis_index("grp")
    core = lax.rem(blk, 2)
    x = lax.rem(lax.div(blk, 2), 4)
    z = lax.div(blk, 8)

    def place(dz, dx, dg):
        zz, xx, gg = lax.rem(z + dz, 4), lax.rem(x + dx, 4), lax.rem(grp + dg, 4)
        return ((zz * 4 + xx) * 2 + core, gg)

    x_dev = (place(0, 1, 0), place(0, 3, 0))
    z_dev = (place(1, 0, 0), place(3, 0, 0))
    y_dev = (place(0, 0, 1), place(0, 0, 3))
    y_far = place(0, 0, 2)
    peer = ((z * 4 + x) * 2 + 1 - core, grp)
    partners = x_dev + z_dev + y_dev + (y_far, peer)

    barrier = pltpu.get_barrier_semaphore()
    for other in partners:
        pl.semaphore_signal(barrier, inc=1, device_id=other, device_id_type=pl.DeviceIdType.MESH)

    loads = [
        pltpu.make_async_copy(source, target, load_sem.at[at])
        for at, (source, target) in enumerate((
            (img_hbm, img_ref), (txt_hbm, txt_ref), (pos_hbm, pos_ref), (cnt_hbm, cnt_ref),
            (row_hbm, row_ref),
        ))
    ]
    for load in loads:
        load.start()
    for load in loads:
        load.wait()

    temper = scale_ref[0]
    offset = bias_ref[0]

    for source, unit, norm in ((img_ref, img, norm_img), (txt_ref, txt, norm_txt)):
        values = source[...]
        length = jnp.sqrt(jnp.sum(values * values, axis=1, keepdims=True) + 1e-06)
        norm[...] = length
        unit[0:ROWS, :] = values / length
    meta[0, 0:4, :] = pos_ref[...]
    meta[0, 4:5, :] = cnt_ref[...]
    meta[0, 5:6, :] = row_ref[...]
    meta[0, 6:8, :] = jnp.zeros((2, ROWS), jnp.int32)

    pl.semaphore_wait(barrier, len(partners))

    copies = {}

    def push(name, source, target, device):
        at = len(copies)
        copy = pltpu.make_async_remote_copy(
            src_ref=source, dst_ref=target, send_sem=send_sem.at[at], recv_sem=recv_sem.at[at],
            device_id=device, device_id_type=pl.DeviceIdType.MESH,
        )
        copy.start()
        copies[name] = copy

    def arrived(name):
        copies[name].wait_recv()

    rings = {"x": (img, 2 * ROWS, x_dev), "z": (txt, ROWS, z_dev)}

    def gather(axis, step, side, part):
        buffer, stride, devices = rings[axis]
        first = {1: side * HALF, 2: stride + side * HALF, 3: (1 - side) * HALF}[step]
        push(
            (axis, step, side, part),
            buffer.at[rows_at(first + part * PIECE, PIECE)],
            buffer.at[rows_at(stride * step + side * HALF + part * PIECE, PIECE)],
            devices[side],
        )

    y_rings = {"yt": (txt, y_txt), "yi": (img, y_img)}

    def gather_y(axis, step, side):
        own, others = y_rings[axis]
        half = side if step != 2 else 1 - side
        if step == 3:
            source = others.at[rows_at(side * ROWS + side * HALF, HALF)]
            target = others.at[rows_at(2 * ROWS + side * HALF, HALF)]
        else:
            source = own.at[rows_at(half * HALF, HALF)]
            target = others.at[rows_at(side * ROWS + half * HALF, HALF)]
        push((axis, step, side), source, target, y_dev[side])

    def across(step):
        first = 2 * ROWS * step
        push(("c", step), img.at[rows_at(first, ROWS)], img.at[rows_at(first + ROWS, ROWS)], peer)

    def split_rows(source, high, low, first, count):
        for at in range(first, first + count, HALF):
            high[at:at + HALF, :], low[at:at + HALF, :] = split(source[at:at + HALF, :])

    def sigmoids(row, rows, col, cols):
        def one(at, count):
            a_hi, a_lo = img_hi[rows_at(at, count), :], img_lo[rows_at(at, count), :]
            b_hi, b_lo = txt_hi[col:col + cols, :], txt_lo[col:col + cols, :]
            dots = dot_nt(a_hi, b_hi) + (dot_nt(a_hi, b_lo) + dot_nt(a_lo, b_hi))
            sig[rows_at(at, count), col:col + cols] = jax.nn.sigmoid(temper * dots + offset)

        if rows <= 256:
            one(row, rows)
        else:
            def turn(i, carry):
                one(pl.multiple_of(row + i * 256, 256), 256)
                return carry

            lax.fori_loop(0, rows // 256, turn, 0)

    def times(left, high, low, store):
        l_hi, l_lo = split(left)
        for at, count in COLS:
            cs = slice(at, at + count)
            store(cs, dot_nn(l_hi, high[:, cs]) + (dot_nn(l_hi, low[:, cs]) + dot_nn(l_lo, high[:, cs])))

    def image_grads(first, col=0, cols=4 * ROWS, add=False):
        def store(cs, value):
            g_img[first:first + ROWS, cs] = g_img[first:first + ROWS, cs] + value if add else value

        times(sig[first:first + ROWS, col:col + cols], txt_hi.at[col:col + cols], txt_lo.at[col:col + cols], store)

    def text_grads(first, row=0, rows=8 * ROWS, add=False):
        def store(cs, value):
            g_txt[first:first + ROWS, cs] = g_txt[first:first + ROWS, cs] + value if add else value

        times(sig[row:row + rows, first:first + ROWS].T, img_hi.at[row:row + rows], img_lo.at[row:row + rows], store)

    for slot, device in ((1, y_dev[0]), (2, y_dev[1]), (3, y_far)):
        push(("m", slot), meta.at[0], meta.at[slot], device)
    for part in (0, 1):
        for axis in ("x", "z"):
            for side in (0, 1):
                gather(axis, 1, side, part)
    across(0)
    for step in (1, 2):
        for side in (0, 1):
            gather_y("yt", step, side)

    split_rows(img, img_hi, img_lo, 0, ROWS)
    split_rows(txt, txt_hi, txt_lo, 0, ROWS)
    arrived(("c", 0))
    split_rows(img, img_hi, img_lo, ROWS, ROWS)
    sigmoids(0, 256, 0, ROWS)

    for slot in (1, 2, 3):
        arrived(("m", slot))
    group_base = blk * (4 * ROWS)
    places = [lax.rem(grp + shift, 4) * ROWS + group_base for shift in (0, 3, 1, 2)]
    tall = lax.broadcasted_iota(jnp.int32, (ROWS, ROWS), 0)

    def named(slot):
        tiles = []
        for ids in range(4):
            hit = None
            for k in range(4):
                listed = jnp.where(meta[slot, 4:5, :] > k, meta[slot, k:k + 1, :], -1)
                same = listed == tall + places[ids]
                hit = same if hit is None else hit | same
            tiles.append(jnp.where(hit, 1.0, 0.0).astype(BF16))
        return jnp.concatenate(tiles, axis=0)

    def held(slot):
        tiles = [
            jnp.where(meta[ids, 5:6, :] == tall + places[slot], 1.0, 0.0).astype(BF16)
            for ids in range(4)
        ]
        return jnp.concatenate(tiles, axis=1)

    for axis in ("x", "z"):
        for side in (0, 1):
            arrived((axis, 1, side, 0))
            gather(axis, 2, side, 0)

    own_ids, own_held = named(0), held(0)
    mark_a[:, 0:ROWS] = dot_nn(own_held, own_ids)
    for slot in (1, 2, 3):
        mark_a[:, slot * ROWS:(slot + 1) * ROWS] = dot_nn(own_held, named(slot))
        mark_b[(slot - 1) * ROWS:slot * ROWS, :] = dot_nn(held(slot), own_ids)

    for axis in ("x", "z"):
        for side in (0, 1):
            arrived((axis, 1, side, 1))
            gather(axis, 2, side, 1)
    across(1)
    for part in (0, 1):
        for axis in ("x", "z"):
            for side in (0, 1):
                gather(axis, 3, side, part)
    for side in (0, 1):
        arrived(("yt", 1, side))
        gather_y("yt", 3, side)
    for step in (1, 2):
        for side in (0, 1):
            gather_y("yi", step, side)

    split_rows(txt, txt_hi, txt_lo, ROWS, ROWS)
    split_rows(img, img_hi, img_lo, 256, ROWS)
    sigmoids(0, 256, ROWS, ROWS)
    arrived(("c", 1))
    split_rows(img, img_hi, img_lo, 256 + ROWS, ROWS)
    sigmoids(256, 256, 0, 256)

    for part in (0, 1):
        for axis in ("x", "z"):
            for side in (0, 1):
                arrived((axis, 2, side, part))
    across(2)
    split_rows(txt, txt_hi, txt_lo, 2 * ROWS, ROWS)
    split_rows(img, img_hi, img_lo, 512, ROWS)
    sigmoids(0, 512, 2 * ROWS, ROWS)
    arrived(("c", 2))
    split_rows(img, img_hi, img_lo, 512 + ROWS, ROWS)
    sigmoids(512, 256, 0, 3 * ROWS)
    text_grads(2 * ROWS, 0, 768)
    image_grads(512 + ROWS, 0, 3 * ROWS)
    image_grads(512, 0, 3 * ROWS)

    for part in (0, 1):
        for side in (0, 1):
            arrived(("x", 3, side, part))
    across(3)
    for part in (0, 1):
        for side in (0, 1):
            arrived(("z", 3, side, part))

    def share(step):
        first = 2 * ROWS * step
        push(("r", step), g_img.at[rows_at(first + ROWS, ROWS)], c_in.at[step], peer)

    def joined(step):
        first = 2 * ROWS * step
        arrived(("r", step))
        g_img[first:first + ROWS, :] += c_in[step]

    scatters = {"x": (g_img, 2 * ROWS, x_dev, x_in), "z": (g_txt, ROWS, z_dev, z_in)}

    def scatter(axis, turn):
        buffer, stride, devices, inbox = scatters[axis]
        for side in (0, 1):
            first = (2 * stride + side * HALF, stride + (1 - side) * HALF, 3 * stride + (1 - side) * HALF)[turn]
            if turn == 2:
                arrived((axis, "s", 0, side))
                buffer[first:first + HALF, :] += inbox[side, 0]
            push((axis, "s", turn, side), buffer.at[rows_at(first, HALF)], inbox.at[side, turn], devices[side])

    split_rows(txt, txt_hi, txt_lo, 3 * ROWS, ROWS)
    sigmoids(512, 256, 3 * ROWS, ROWS)
    image_grads(512 + ROWS, 3 * ROWS, ROWS, True)
    share(2)
    image_grads(512, 3 * ROWS, ROWS, True)
    split_rows(img, img_hi, img_lo, 768, ROWS)
    arrived(("c", 3))
    split_rows(img, img_hi, img_lo, 768 + ROWS, ROWS)
    sigmoids(768, 256, 2 * ROWS, ROWS)
    text_grads(2 * ROWS, 768, 256, True)
    scatter("z", 0)
    joined(2)
    scatter("x", 0)

    sigmoids(0, 512, 3 * ROWS, ROWS)
    image_grads(256 + ROWS)
    share(1)
    image_grads(256)
    sigmoids(768, 256, 0, 2 * ROWS)
    joined(1)
    scatter("x", 1)
    text_grads(ROWS)
    scatter("z", 1)

    for side in (0, 1):
        arrived(("yi", 1, side))
        gather_y("yi", 3, side)

    sigmoids(768, 256, 3 * ROWS, ROWS)
    image_grads(768 + ROWS)
    share(3)
    image_grads(768)
    text_grads(3 * ROWS)
    joined(3)
    scatter("x", 2)
    scatter("z", 2)

    image_grads(ROWS)
    share(0)
    sig[0:ROWS, 0:ROWS] -= mark_a[:, 0:ROWS]
    image_grads(0)
    text_grads(0)

    for side in (0, 1):
        arrived(("yt", 2, side))
        arrived(("yt", 3, side))
    split_rows(y_txt, yt_hi, yt_lo, 0, 3 * ROWS)
    own = rows_at(0, ROWS)
    dots = dot_nt(img_hi[own, :], yt_hi[...]) + (dot_nt(img_hi[own, :], yt_lo[...]) + dot_nt(img_lo[own, :], yt_hi[...]))
    coef = mark_a[:, ROWS:4 * ROWS] * (jax.nn.sigmoid(temper * dots + offset) - 1.0)

    def add_img(cs, value):
        g_img[0:ROWS, cs] += value

    times(coef, yt_hi, yt_lo, add_img)
    joined(0)

    for side in (0, 1):
        arrived(("yi", 2, side))
        arrived(("yi", 3, side))
    split_rows(y_img, yi_hi, yi_lo, 0, 3 * ROWS)
    dots = dot_nt(yi_hi[...], txt_hi[own, :]) + (dot_nt(yi_hi[...], txt_lo[own, :]) + dot_nt(yi_lo[...], txt_hi[own, :]))
    coef = mark_b[...] * (jax.nn.sigmoid(temper * dots + offset) - 1.0)

    def add_txt(cs, value):
        g_txt[0:ROWS, cs] += value

    times(coef.T, yi_hi, yi_lo, add_txt)

    ends = (
        ("x", g_img, x_in, img, norm_img, gimg_ref),
        ("z", g_txt, z_in, txt, norm_txt, gtxt_ref),
    )
    for axis, sums, inbox, unit, norm, out in ends:
        for side in (0, 1):
            at = slice((1 - side) * HALF, (2 - side) * HALF)
            arrived((axis, "s", 1, side))
            sums[at, :] += inbox[side, 1]
    for axis, sums, inbox, unit, norm, out in ends:
        for side in (0, 1):
            arrived((axis, "s", 2, side))
        for half in (0, 1):
            at = slice(half * HALF, (half + 1) * HALF)
            grad = temper * (sums[at, :] + inbox[half, 2])
            units = unit[at, :]
            along = jnp.sum(units * grad, axis=1, keepdims=True)
            out[at, :] = (grad - units * along) / norm[at, :]

    for copy in copies.values():
        copy.wait_send()


def hand_on(gimg_in, gtxt_in, gimg_out, gtxt_out, sems):
    copies = [
        pltpu.make_async_copy(gimg_in, gimg_out, sems.at[0]),
        pltpu.make_async_copy(gtxt_in, gtxt_out, sems.at[1]),
    ]
    for copy in copies:
        copy.start()
    for copy in copies:
        copy.wait()


def body(image_emb, text_emb, logit_scale, logit_bias, pos_image, pos_count, image_row):
    anywhere = pl.BlockSpec(memory_space=pl.ANY)
    vmem = pl.BlockSpec(memory_space=pltpu.VMEM)
    rows = jax.ShapeDtypeStruct((ROWS, D), F32)
    grads = pl.pallas_call(
        kernel,
        out_shape=(pltpu.VMEM((ROWS, D), F32), pltpu.VMEM((ROWS, D), F32)),
        in_specs=[pl.BlockSpec(memory_space=pltpu.SMEM)] * 2 + [pl.BlockSpec(memory_space=pltpu.HBM)] * 5,
        out_specs=(vmem, vmem),
        scratch_shapes=[
            pltpu.VMEM((ROWS, D), F32),
            pltpu.VMEM((ROWS, D), F32),
            pltpu.VMEM((4, ROWS), jnp.int32),
            pltpu.VMEM((1, ROWS), jnp.int32),
            pltpu.VMEM((1, ROWS), jnp.int32),
            pltpu.SemaphoreType.DMA((5,)),
            pltpu.VMEM((8 * ROWS, D), F32),
            pltpu.VMEM((4 * ROWS, D), F32),
            pltpu.VMEM((8 * ROWS, D), BF16),
            pltpu.VMEM((8 * ROWS, D), BF16),
            pltpu.VMEM((4 * ROWS, D), BF16),
            pltpu.VMEM((4 * ROWS, D), BF16),
            pltpu.VMEM((8 * ROWS, 4 * ROWS), F32),
            pltpu.VMEM((8 * ROWS, D), F32),
            pltpu.VMEM((4 * ROWS, D), F32),
            pltpu.VMEM((3 * ROWS, D), F32),
            pltpu.VMEM((3 * ROWS, D), F32),
            pltpu.VMEM((3 * ROWS, D), BF16),
            pltpu.VMEM((3 * ROWS, D), BF16),
            pltpu.VMEM((3 * ROWS, D), BF16),
            pltpu.VMEM((3 * ROWS, D), BF16),
            pltpu.VMEM((2, 3, HALF, D), F32),
            pltpu.VMEM((2, 3, HALF, D), F32),
            pltpu.VMEM((4, ROWS, D), F32),
            pltpu.VMEM((4, 8, ROWS), jnp.int32),
            pltpu.VMEM((ROWS, 4 * ROWS), F32),
            pltpu.VMEM((3 * ROWS, ROWS), F32),
            pltpu.VMEM((ROWS, 1), F32),
            pltpu.VMEM((ROWS, 1), F32),
            pltpu.SemaphoreType.DMA((N_COPIES,)),
            pltpu.SemaphoreType.DMA((N_COPIES,)),
        ],
        compiler_params=pltpu.CompilerParams(
            collective_id=0, has_side_effects=True, vmem_limit_bytes=42 * 2**20
        ),
        name="align_step",
    )(
        logit_scale,
        logit_bias,
        *(
            pltpu.with_memory_space_constraint(operand, pltpu.HBM)
            for operand in (
                image_emb, text_emb, pos_image.T, pos_count.reshape(1, ROWS), image_row.reshape(1, ROWS),
            )
        ),
    )
    grads = [pltpu.with_memory_space_constraint(grad, pltpu.VMEM) for grad in grads]
    return pl.pallas_call(
        hand_on,
        out_shape=(rows, rows),
        in_specs=[vmem, vmem],
        out_specs=(anywhere, anywhere),
        scratch_shapes=[pltpu.SemaphoreType.DMA((2,))],
        name="hand_on",
    )(*grads)


def solution(mesh):
    return jax.shard_map(
        body,
        mesh=mesh,
        in_specs=(
            P(("blk", "grp"), None),
            P(("blk", "grp"), None),
            P(),
            P(),
            P(("blk", "grp"), None),
            P(("blk", "grp")),
            P(("blk", "grp")),
        ),
        out_specs=(P(("blk", "grp"), None), P(("blk", "grp"), None)),
        check_vma=False,
    )
```

```python
import functools

import jax
import jax.numpy as jnp
from jax import lax
from jax.experimental import pallas as pl
from jax.experimental.pallas import tpu as pltpu
from jax.sharding import PartitionSpec as P

ROWS = 128
HALF = 64
PIECE = 32
D = 1152
COLS = ((0, 256), (256, 256), (512, 256), (768, 256), (1024, 128))
N_SEND = 5
N_RECV = 33
CORE, GATHER, ALONG_Y, SCATTER, LISTS = range(N_SEND)
F32 = jnp.float32
BF16 = jnp.bfloat16


def rows_at(start, count):
    return pl.ds(start, count)


def split(values):
    high = values.astype(BF16)
    return high, (values - high.astype(F32)).astype(BF16)


def dot_nn(a, b):
    return lax.dot_general(a, b, (((1,), (0,)), ((), ())), preferred_element_type=F32)


def dot_nt(a, b):
    return lax.dot_general(a, b, (((1,), (1,)), ((), ())), preferred_element_type=F32)


def kernel(
    scale_ref, bias_ref, img_hbm, txt_hbm, pos_hbm, cnt_hbm, row_hbm,
    gimg_ref, gtxt_ref,
    img_ref, txt_ref, pos_ref, cnt_ref, row_ref, load_sem,
    img, txt, img_hi, img_lo, txt_hi, txt_lo, sig, g_img, g_txt,
    y_txt, y_img, yt_hi, yt_lo, yi_hi, yi_lo,
    txt_both, x_in, z_in, c_in, meta, mark_a, mark_b, norm_img, norm_txt, send_sem, recv_sem,
):
    blk, grp = lax.axis_index("blk"), lax.axis_index("grp")
    core = lax.rem(blk, 2)
    x = lax.rem(lax.div(blk, 2), 4)
    z = lax.div(blk, 8)

    def place(dz, dx, dg):
        zz, xx, gg = lax.rem(z + dz, 4), lax.rem(x + dx, 4), lax.rem(grp + dg, 4)
        return ((zz * 4 + xx) * 2 + core, gg)

    x_dev = (place(0, 1, 0), place(0, 3, 0))
    z_dev = (place(1, 0, 0), place(3, 0, 0))
    y_dev = (place(0, 0, 1), place(0, 0, 3))
    y_far = place(0, 0, 2)
    peer = ((z * 4 + x) * 2 + 1 - core, grp)
    partners = x_dev + z_dev + y_dev + (y_far, peer)

    barrier = pltpu.get_barrier_semaphore()
    for other in partners:
        pl.semaphore_signal(barrier, inc=1, device_id=other, device_id_type=pl.DeviceIdType.MESH)

    temper = scale_ref[0]
    offset = bias_ref[0]
    sources = ((img_hbm, img_ref, img, norm_img), (txt_hbm, txt_ref, txt, norm_txt))
    for part in (0, 1):
        for hbm, ref, _, _ in sources:
            for half in (0, 1):
                at = rows_at(half * HALF + part * PIECE, PIECE)
                pltpu.make_async_copy(hbm.at[at], ref.at[at], load_sem.at[part]).start()
    small = [
        pltpu.make_async_copy(source, target, load_sem.at[2 + at])
        for at, (source, target) in enumerate(((pos_hbm, pos_ref), (cnt_hbm, cnt_ref), (row_hbm, row_ref)))
    ]
    for load in small:
        load.start()

    def normalize(part):
        pltpu.make_async_copy(img_hbm, img_ref, load_sem.at[part]).wait()
        for _, ref, unit, norm in sources:
            for half in (0, 1):
                at = rows_at(half * HALF + part * PIECE, PIECE)
                values = ref[at, :]
                length = jnp.sqrt(jnp.sum(values * values, axis=1, keepdims=True) + 1e-06)
                norm[at, :] = length
                unit[at, :] = values / length

    normalize(0)
    pl.semaphore_wait(barrier, len(partners))

    groups = {}

    def push(group, source, target, device, send):
        at = groups.setdefault(group, len(groups))
        pltpu.make_async_remote_copy(
            src_ref=source, dst_ref=target, send_sem=send_sem.at[send], recv_sem=recv_sem.at[at],
            device_id=device, device_id_type=pl.DeviceIdType.MESH,
        ).start()

    def done(sem, region):
        pltpu.make_async_copy(region, region, sem).wait()

    def arrived(group, region):
        done(recv_sem.at[groups[group]], region)

    rings = {"x": (img, 2 * ROWS, x_dev), "z": (txt, ROWS, z_dev)}

    def piece(axis, step, side, part):
        buffer, stride, _ = rings[axis]
        return buffer.at[rows_at(stride * step + side * HALF + part * PIECE, PIECE)]

    def gather(axis, step, side, part):
        buffer, stride, devices = rings[axis]
        first = {1: side * HALF, 2: stride + side * HALF, 3: (1 - side) * HALF}[step]
        push(
            (axis, 1, side, part) if step == 1 else (axis, step),
            buffer.at[rows_at(first + part * PIECE, PIECE)],
            piece(axis, step, side, part),
            devices[side],
            GATHER,
        )

    def gathered(axis, step):
        buffer, stride, _ = rings[axis]
        arrived((axis, step), buffer.at[rows_at(stride * step, ROWS)])

    y_rings = {"yt": (txt, y_txt), "yi": (img, y_img)}

    def gather_y(axis, step, side):
        own, others = y_rings[axis]
        half = side if step != 2 else 1 - side
        if step == 3:
            source = others.at[rows_at(side * ROWS + side * HALF, HALF)]
            target = others.at[rows_at(2 * ROWS + side * HALF, HALF)]
        else:
            source = own.at[rows_at(half * HALF, HALF)]
            target = others.at[rows_at(side * ROWS + half * HALF, HALF)]
        push((axis, 1, side) if step == 1 else (axis, 2), source, target, y_dev[side], ALONG_Y)

    def forward_y(axis):
        others = y_rings[axis][1]
        for side in (0, 1):
            arrived((axis, 1, side), others.at[rows_at(side * ROWS + side * HALF, HALF)])
            gather_y(axis, 3, side)

    def across(step):
        first = 2 * ROWS * step
        push(("c", step), img.at[rows_at(first, ROWS)], img.at[rows_at(first + ROWS, ROWS)], peer, CORE)

    def crossed(step):
        arrived(("c", step), img.at[rows_at(2 * ROWS * step + ROWS, ROWS)])

    def split_rows(source, high, low, first, count):
        for at in range(first, first + count, HALF):
            high[at:at + HALF, :], low[at:at + HALF, :] = split(source[at:at + HALF, :])

    def split_img(first):
        split_rows(img, img_hi, img_lo, first, ROWS)

    def split_txt(step):
        for at in range(ROWS * step, ROWS * (step + 1), HALF):
            high, low = split(txt[at:at + HALF, :])
            txt_hi[at:at + HALF, :] = high
            txt_lo[at:at + HALF, :] = low
            both = at + ROWS * step
            txt_both[both:both + HALF, :] = high
            txt_both[both + ROWS:both + ROWS + HALF, :] = low

    def sigmoids(row, rows, col, cols):
        def one(at, count):
            a_hi, a_lo = img_hi[rows_at(at, count), :], img_lo[rows_at(at, count), :]
            wide = cols - cols % 256
            if wide:
                b_hi, b_lo = txt_hi[col:col + wide, :], txt_lo[col:col + wide, :]
                dots = dot_nt(a_hi, b_hi) + (dot_nt(a_hi, b_lo) + dot_nt(a_lo, b_hi))
                sig[rows_at(at, count), col:col + wide] = jax.nn.sigmoid(temper * dots + offset)
            if cols % 256:
                last = col + wide
                both = dot_nt(a_hi, txt_both[2 * last:2 * last + 2 * ROWS, :])
                dots = both[:, :ROWS] + (both[:, ROWS:] + dot_nt(a_lo, txt_hi[last:last + ROWS, :]))
                sig[rows_at(at, count), last:last + ROWS] = jax.nn.sigmoid(temper * dots + offset)

        if rows <= 256:
            one(row, rows)
        else:
            def turn(i, carry):
                one(pl.multiple_of(row + i * 256, 256), 256)
                return carry

            lax.fori_loop(0, rows // 256, turn, 0)

    def times(left, high, low, store):
        l_hi, l_lo = split(left)
        for at, count in COLS:
            cs = slice(at, at + count)
            store(cs, dot_nn(l_hi, high[:, cs]) + (dot_nn(l_hi, low[:, cs]) + dot_nn(l_lo, high[:, cs])))

    def image_grads(first, cols=4 * ROWS):
        def store(cs, value):
            g_img[first:first + ROWS, cs] = value

        times(sig[first:first + ROWS, 0:cols], txt_hi.at[0:cols], txt_lo.at[0:cols], store)

    def add_image_grads(first, step):
        s_hi, s_lo = split(sig[first:first + ROWS, ROWS * step:ROWS * (step + 1)])
        s_hi = jnp.concatenate([s_hi, s_hi], axis=1)
        for at, count in COLS:
            cs = slice(at, at + count)
            g_img[first:first + ROWS, cs] += (
                dot_nn(s_hi, txt_both[2 * ROWS * step:2 * ROWS * (step + 1), cs])
                + dot_nn(s_lo, txt_hi[ROWS * step:ROWS * (step + 1), cs])
            )

    def text_grads(first, row=0, rows=8 * ROWS, add=False):
        def store(cs, value):
            g_txt[first:first + ROWS, cs] = g_txt[first:first + ROWS, cs] + value if add else value

        times(sig[row:row + rows, first:first + ROWS].T, img_hi.at[row:row + rows], img_lo.at[row:row + rows], store)

    for axis in ("x", "z"):
        for side in (0, 1):
            gather(axis, 1, side, 0)
    normalize(1)
    for axis in ("x", "z"):
        for side in (0, 1):
            gather(axis, 1, side, 1)
    across(0)
    for load in small:
        load.wait()
    meta[0, 0:4, :] = pos_ref[...]
    meta[0, 4:5, :] = cnt_ref[...]
    meta[0, 5:6, :] = row_ref[...]
    meta[0, 6:8, :] = jnp.zeros((2, ROWS), jnp.int32)
    for slot, device in ((1, y_dev[0]), (2, y_dev[1]), (3, y_far)):
        push("m", meta.at[0], meta.at[slot], device, LISTS)
    for step in (1, 2):
        for side in (0, 1):
            gather_y("yt", step, side)

    split_img(0)
    split_txt(0)
    crossed(0)
    split_img(ROWS)
    sigmoids(0, 256, 0, ROWS)

    arrived("m", meta.at[1:4])
    group_base = blk * (4 * ROWS)
    places = [lax.rem(grp + shift, 4) * ROWS + group_base for shift in (0, 3, 1, 2)]
    tall = lax.broadcasted_iota(jnp.int32, (ROWS, ROWS), 0)

    def named(slot):
        tiles = []
        for ids in range(4):
            hit = None
            for k in range(4):
                listed = jnp.where(meta[slot, 4:5, :] > k, meta[slot, k:k + 1, :], -1)
                same = listed == tall + places[ids]
                hit = same if hit is None else hit | same
            tiles.append(jnp.where(hit, 1.0, 0.0).astype(BF16))
        return jnp.concatenate(tiles, axis=0)

    def held(slot):
        tiles = [
            jnp.where(meta[ids, 5:6, :] == tall + places[slot], 1.0, 0.0).astype(BF16)
            for ids in range(4)
        ]
        return jnp.concatenate(tiles, axis=1)

    for axis in ("x", "z"):
        for side in (0, 1):
            arrived((axis, 1, side, 0), piece(axis, 1, side, 0))
            gather(axis, 2, side, 0)

    own_ids, own_held = named(0), held(0)
    mark_a[:, 0:ROWS] = dot_nn(own_held, own_ids)
    for slot in (1, 2, 3):
        mark_a[:, slot * ROWS:(slot + 1) * ROWS] = dot_nn(own_held, named(slot))
        mark_b[(slot - 1) * ROWS:slot * ROWS, :] = dot_nn(held(slot), own_ids)

    for axis in ("x", "z"):
        for side in (0, 1):
            arrived((axis, 1, side, 1), piece(axis, 1, side, 1))
            gather(axis, 2, side, 1)
    across(1)
    for part in (0, 1):
        for axis in ("x", "z"):
            for side in (0, 1):
                gather(axis, 3, side, part)
    forward_y("yt")
    for step in (1, 2):
        for side in (0, 1):
            gather_y("yi", step, side)

    split_txt(1)
    split_img(256)
    sigmoids(0, 256, ROWS, ROWS)
    sigmoids(256, ROWS, 0, 256)
    crossed(1)
    split_img(256 + ROWS)
    sigmoids(256 + ROWS, ROWS, 0, 256)

    gathered("x", 2)
    across(2)
    gathered("z", 2)
    split_txt(2)
    split_img(512)
    sigmoids(0, 512, 2 * ROWS, ROWS)
    sigmoids(512, ROWS, 0, 3 * ROWS)
    crossed(2)
    split_img(512 + ROWS)
    sigmoids(512 + ROWS, ROWS, 0, 3 * ROWS)
    image_grads(512 + ROWS, 3 * ROWS)
    image_grads(512, 3 * ROWS)
    text_grads(2 * ROWS, 0, 768)

    gathered("x", 3)
    across(3)
    gathered("z", 3)

    def share(step):
        first = 2 * ROWS * step
        push(("r", step), g_img.at[rows_at(first + ROWS, ROWS)], c_in.at[step], peer, CORE)

    def joined(step):
        first = 2 * ROWS * step
        arrived(("r", step), c_in.at[step])
        g_img[first:first + ROWS, :] += c_in[step]

    scatters = {"x": (g_img, 2 * ROWS, x_dev, x_in), "z": (g_txt, ROWS, z_dev, z_in)}

    def scatter(axis, turn):
        buffer, stride, devices, inbox = scatters[axis]
        if turn == 2:
            arrived((axis, "s", 0), inbox.at[0])
        for side in (0, 1):
            first = (2 * stride + side * HALF, stride + (1 - side) * HALF, 3 * stride + (1 - side) * HALF)[turn]
            if turn == 2:
                buffer[first:first + HALF, :] += inbox[0, side]
            push((axis, "s", turn), buffer.at[rows_at(first, HALF)], inbox.at[turn, side], devices[side], SCATTER)

    split_txt(3)
    sigmoids(512 + ROWS, ROWS, 3 * ROWS, ROWS)
    add_image_grads(512 + ROWS, 3)
    share(2)
    sigmoids(512, ROWS, 3 * ROWS, ROWS)
    add_image_grads(512, 3)
    split_img(768)
    sigmoids(768, ROWS, 2 * ROWS, ROWS)
    crossed(3)
    split_img(768 + ROWS)
    sigmoids(768 + ROWS, ROWS, 2 * ROWS, ROWS)
    text_grads(2 * ROWS, 768, 256, True)
    scatter("z", 0)
    joined(2)
    scatter("x", 0)

    sigmoids(0, 512, 3 * ROWS, ROWS)
    image_grads(256 + ROWS)
    share(1)
    image_grads(256)
    sigmoids(768, 256, 0, 2 * ROWS)
    joined(1)
    scatter("x", 1)
    text_grads(ROWS)
    scatter("z", 1)

    forward_y("yi")

    sigmoids(768, 256, 3 * ROWS, ROWS)
    image_grads(768 + ROWS)
    share(3)
    image_grads(768)
    text_grads(3 * ROWS)
    joined(3)
    scatter("x", 2)
    scatter("z", 2)

    image_grads(ROWS)
    share(0)
    sig[0:ROWS, 0:ROWS] -= mark_a[:, 0:ROWS]
    image_grads(0)
    text_grads(0)

    arrived(("yt", 2), y_txt.at[ROWS:3 * ROWS])
    split_rows(y_txt, yt_hi, yt_lo, 0, 3 * ROWS)
    own = rows_at(0, ROWS)
    dots = dot_nt(img_hi[own, :], yt_hi[...]) + (dot_nt(img_hi[own, :], yt_lo[...]) + dot_nt(img_lo[own, :], yt_hi[...]))
    coef = mark_a[:, ROWS:4 * ROWS] * (jax.nn.sigmoid(temper * dots + offset) - 1.0)

    def add_img(cs, value):
        g_img[0:ROWS, cs] += value

    times(coef, yt_hi, yt_lo, add_img)
    joined(0)

    arrived(("yi", 2), y_img.at[ROWS:3 * ROWS])
    split_rows(y_img, yi_hi, yi_lo, 0, 3 * ROWS)
    dots = dot_nt(yi_hi[...], txt_hi[own, :]) + (dot_nt(yi_hi[...], txt_lo[own, :]) + dot_nt(yi_lo[...], txt_hi[own, :]))
    coef = mark_b[...] * (jax.nn.sigmoid(temper * dots + offset) - 1.0)

    def add_txt(cs, value):
        g_txt[0:ROWS, cs] += value

    times(coef.T, yi_hi, yi_lo, add_txt)

    ends = (
        ("x", g_img, x_in, img, norm_img, gimg_ref),
        ("z", g_txt, z_in, txt, norm_txt, gtxt_ref),
    )
    for axis, sums, inbox, unit, norm, out in ends:
        arrived((axis, "s", 1), inbox.at[1])
        for side in (0, 1):
            at = slice((1 - side) * HALF, (2 - side) * HALF)
            sums[at, :] += inbox[1, side]
    for axis, sums, inbox, unit, norm, out in ends:
        arrived((axis, "s", 2), inbox.at[2])
        for half in (0, 1):
            at = slice(half * HALF, (half + 1) * HALF)
            grad = temper * (sums[at, :] + inbox[2, half])
            units = unit[at, :]
            along = jnp.sum(units * grad, axis=1, keepdims=True)
            out[at, :] = (grad - units * along) / norm[at, :]

    done(send_sem.at[CORE], g_img)
    done(send_sem.at[GATHER], g_img.at[0:6 * ROWS])
    done(send_sem.at[ALONG_Y], g_img.at[0:6 * ROWS])
    done(send_sem.at[SCATTER], g_img.at[0:6 * ROWS])
    done(send_sem.at[LISTS], meta.at[1:4])


def hand_on(gimg_in, gtxt_in, gimg_out, gtxt_out, sems):
    copies = [
        pltpu.make_async_copy(gimg_in, gimg_out, sems.at[0]),
        pltpu.make_async_copy(gtxt_in, gtxt_out, sems.at[1]),
    ]
    for copy in copies:
        copy.start()
    for copy in copies:
        copy.wait()


def body(image_emb, text_emb, logit_scale, logit_bias, pos_image, pos_count, image_row):
    anywhere = pl.BlockSpec(memory_space=pl.ANY)
    vmem = pl.BlockSpec(memory_space=pltpu.VMEM)
    rows = jax.ShapeDtypeStruct((ROWS, D), F32)
    grads = pl.pallas_call(
        kernel,
        out_shape=(pltpu.VMEM((ROWS, D), F32), pltpu.VMEM((ROWS, D), F32)),
        in_specs=[pl.BlockSpec(memory_space=pltpu.SMEM)] * 2 + [pl.BlockSpec(memory_space=pltpu.HBM)] * 5,
        out_specs=(vmem, vmem),
        scratch_shapes=[
            pltpu.VMEM((ROWS, D), F32),
            pltpu.VMEM((ROWS, D), F32),
            pltpu.VMEM((4, ROWS), jnp.int32),
            pltpu.VMEM((1, ROWS), jnp.int32),
            pltpu.VMEM((1, ROWS), jnp.int32),
            pltpu.SemaphoreType.DMA((5,)),
            pltpu.VMEM((8 * ROWS, D), F32),
            pltpu.VMEM((4 * ROWS, D), F32),
            pltpu.VMEM((8 * ROWS, D), BF16),
            pltpu.VMEM((8 * ROWS, D), BF16),
            pltpu.VMEM((4 * ROWS, D), BF16),
            pltpu.VMEM((4 * ROWS, D), BF16),
            pltpu.VMEM((8 * ROWS, 4 * ROWS), F32),
            pltpu.VMEM((8 * ROWS, D), F32),
            pltpu.VMEM((4 * ROWS, D), F32),
            pltpu.VMEM((3 * ROWS, D), F32),
            pltpu.VMEM((3 * ROWS, D), F32),
            pltpu.VMEM((3 * ROWS, D), BF16),
            pltpu.VMEM((3 * ROWS, D), BF16),
            pltpu.VMEM((3 * ROWS, D), BF16),
            pltpu.VMEM((3 * ROWS, D), BF16),
            pltpu.VMEM((8 * ROWS, D), BF16),
            pltpu.VMEM((3, 2, HALF, D), F32),
            pltpu.VMEM((3, 2, HALF, D), F32),
            pltpu.VMEM((4, ROWS, D), F32),
            pltpu.VMEM((4, 8, ROWS), jnp.int32),
            pltpu.VMEM((ROWS, 4 * ROWS), F32),
            pltpu.VMEM((3 * ROWS, ROWS), F32),
            pltpu.VMEM((ROWS, 1), F32),
            pltpu.VMEM((ROWS, 1), F32),
            pltpu.SemaphoreType.DMA((N_SEND,)),
            pltpu.SemaphoreType.DMA((N_RECV,)),
        ],
        compiler_params=pltpu.CompilerParams(
            collective_id=0, has_side_effects=True, vmem_limit_bytes=46 * 2**20
        ),
        name="align_step",
    )(
        logit_scale,
        logit_bias,
        *(
            pltpu.with_memory_space_constraint(operand, pltpu.HBM)
            for operand in (
                image_emb, text_emb, pos_image.T, pos_count.reshape(1, ROWS), image_row.reshape(1, ROWS),
            )
        ),
    )
    grads = [pltpu.with_memory_space_constraint(grad, pltpu.VMEM) for grad in grads]
    return pl.pallas_call(
        hand_on,
        out_shape=(rows, rows),
        in_specs=[anywhere, anywhere],
        out_specs=(anywhere, anywhere),
        scratch_shapes=[pltpu.SemaphoreType.DMA((2,))],
        name="hand_on",
    )(*grads)


def solution(mesh):
    return jax.shard_map(
        body,
        mesh=mesh,
        in_specs=(
            P(("blk", "grp"), None),
            P(("blk", "grp"), None),
            P(),
            P(),
            P(("blk", "grp"), None),
            P(("blk", "grp")),
            P(("blk", "grp")),
        ),
        out_specs=(P(("blk", "grp"), None), P(("blk", "grp"), None)),
        check_vma=False,
    )
```

```python
import functools

import jax
import jax.numpy as jnp
from jax import lax
from jax.experimental import pallas as pl
from jax.experimental.pallas import tpu as pltpu
from jax.sharding import PartitionSpec as P

ROWS = 128
HALF = 64
PIECE = 32
D = 1152
COLS = ((0, 256), (256, 256), (512, 256), (768, 256), (1024, 128))
N_SEND = 5
N_RECV = 36
CORE, GATHER, ALONG_Y, SCATTER, LISTS = range(N_SEND)
F32 = jnp.float32
BF16 = jnp.bfloat16


def rows_at(start, count):
    return pl.ds(start, count)


def split(values):
    high = values.astype(BF16)
    return high, (values - high.astype(F32)).astype(BF16)


def dot_nn(a, b):
    return lax.dot_general(a, b, (((1,), (0,)), ((), ())), preferred_element_type=F32)


def dot_nt(a, b):
    return lax.dot_general(a, b, (((1,), (1,)), ((), ())), preferred_element_type=F32)


def kernel(
    scale_ref, bias_ref, img_hbm, txt_hbm, pos_hbm, cnt_hbm, row_hbm,
    gimg_ref, gtxt_ref,
    img_ref, txt_ref, pos_ref, cnt_ref, row_ref, load_sem,
    img, txt, img_hi, img_lo, txt_hi, txt_lo, sig, g_img, g_txt,
    y_txt, y_img, yt_hi, yt_lo, yi_hi, yi_lo,
    txt_both, x_in, z_in, x_far, z_far, c_in, meta, mark_a, mark_b, norm_img, norm_txt, send_sem, recv_sem,
):
    blk, grp = lax.axis_index("blk"), lax.axis_index("grp")
    core = lax.rem(blk, 2)
    x = lax.rem(lax.div(blk, 2), 4)
    z = lax.div(blk, 8)

    def place(dz, dx, dg):
        zz, xx, gg = lax.rem(z + dz, 4), lax.rem(x + dx, 4), lax.rem(grp + dg, 4)
        return ((zz * 4 + xx) * 2 + core, gg)

    x_dev = (place(0, 1, 0), place(0, 3, 0))
    z_dev = (place(1, 0, 0), place(3, 0, 0))
    y_dev = (place(0, 0, 1), place(0, 0, 3))
    y_far = place(0, 0, 2)
    peer = ((z * 4 + x) * 2 + 1 - core, grp)
    partners = x_dev + z_dev + y_dev + (y_far, peer)

    barrier = pltpu.get_barrier_semaphore()
    for other in partners:
        pl.semaphore_signal(barrier, inc=1, device_id=other, device_id_type=pl.DeviceIdType.MESH)

    temper = scale_ref[0]
    offset = bias_ref[0]
    sources = ((img_hbm, img_ref, img, norm_img), (txt_hbm, txt_ref, txt, norm_txt))

    def load(part):
        for hbm, ref, _, _ in sources:
            for half in (0, 1):
                at = rows_at(half * HALF + part * PIECE, PIECE)
                pltpu.make_async_copy(hbm.at[at], ref.at[at], load_sem.at[part]).start()

    def loaded(part):
        pltpu.make_async_copy(img_hbm, img_ref, load_sem.at[part]).wait()

    load(0)
    small = [
        pltpu.make_async_copy(source, target, load_sem.at[2 + at])
        for at, (source, target) in enumerate(((pos_hbm, pos_ref), (cnt_hbm, cnt_ref), (row_hbm, row_ref)))
    ]
    for each in small:
        each.start()

    def normalize(part):
        for _, ref, unit, norm in sources:
            for half in (0, 1):
                at = rows_at(half * HALF + part * PIECE, PIECE)
                values = ref[at, :]
                length = jnp.sqrt(jnp.sum(values * values, axis=1, keepdims=True) + 1e-06)
                norm[at, :] = length
                unit[at, :] = values / length

    loaded(0)
    load(1)
    normalize(0)
    pl.semaphore_wait(barrier, len(partners))

    groups = {}

    def push(group, source, target, device, send):
        at = groups.setdefault(group, len(groups))
        pltpu.make_async_remote_copy(
            src_ref=source, dst_ref=target, send_sem=send_sem.at[send], recv_sem=recv_sem.at[at],
            device_id=device, device_id_type=pl.DeviceIdType.MESH,
        ).start()

    def done(sem, region):
        pltpu.make_async_copy(region, region, sem).wait()

    def arrived(group, region):
        done(recv_sem.at[groups[group]], region)

    rings = {"x": (img, 2 * ROWS, x_dev), "z": (txt, ROWS, z_dev)}

    def place_of(axis, step, side, part):
        stride = rings[axis][1]
        if step == 3:
            return 3 * stride + part * (stride // 2) + side * PIECE
        return stride * step + side * HALF + part * PIECE

    def gather(axis, step, side, part):
        buffer, stride, devices = rings[axis]
        first = {1: side * HALF, 2: (1 - side) * HALF, 3: stride + side * HALF}[step]
        push(
            {1: (axis, 1, side), 2: (axis, 2), 3: (axis, 3, part)}[step],
            buffer.at[rows_at(first + part * PIECE, PIECE)],
            buffer.at[rows_at(place_of(axis, step, side, part), PIECE)],
            devices[side],
            GATHER,
        )

    def near(axis, side):
        buffer, stride, _ = rings[axis]
        arrived((axis, 1, side), buffer.at[rows_at(stride + side * HALF, HALF)])

    def near_rest(axis):
        buffer, stride, _ = rings[axis]
        arrived((axis, 2), buffer.at[rows_at(2 * stride, ROWS)])

    def far(axis, part):
        buffer, stride, _ = rings[axis]
        arrived((axis, 3, part), buffer.at[rows_at(3 * stride + part * (stride // 2), HALF)])

    y_rings = {"yt": (txt, y_txt), "yi": (img, y_img)}

    def gather_y(axis, step, side):
        own, others = y_rings[axis]
        half = side if step != 2 else 1 - side
        if step == 3:
            source = others.at[rows_at(side * ROWS + side * HALF, HALF)]
            target = others.at[rows_at(2 * ROWS + side * HALF, HALF)]
        else:
            source = own.at[rows_at(half * HALF, HALF)]
            target = others.at[rows_at(side * ROWS + half * HALF, HALF)]
        push((axis, 1, side) if step == 1 else (axis, 2), source, target, y_dev[side], ALONG_Y)

    def forward_y(axis):
        others = y_rings[axis][1]
        for side in (0, 1):
            arrived((axis, 1, side), others.at[rows_at(side * ROWS + side * HALF, HALF)])
            gather_y(axis, 3, side)

    def across(step):
        first = 2 * ROWS * step
        push(("c", step), img.at[rows_at(first, ROWS)], img.at[rows_at(first + ROWS, ROWS)], peer, CORE)

    def crossed(step):
        arrived(("c", step), img.at[rows_at(2 * ROWS * step + ROWS, ROWS)])

    def across_far(part):
        first = 6 * ROWS + part * ROWS
        push(("c", 3, part), img.at[rows_at(first, HALF)], img.at[rows_at(first + HALF, HALF)], peer, CORE)

    def crossed_far(part):
        arrived(("c", 3, part), img.at[rows_at(6 * ROWS + part * ROWS + HALF, HALF)])

    def split_rows(source, high, low, first, count):
        for at in range(first, first + count, HALF):
            high[at:at + HALF, :], low[at:at + HALF, :] = split(source[at:at + HALF, :])

    def split_img(first, count=ROWS):
        split_rows(img, img_hi, img_lo, first, count)

    def split_txt(step, first=0, count=ROWS):
        for at in range(ROWS * step + first, ROWS * step + first + count, HALF):
            high, low = split(txt[at:at + HALF, :])
            txt_hi[at:at + HALF, :] = high
            txt_lo[at:at + HALF, :] = low
            both = at + ROWS * step
            txt_both[both:both + HALF, :] = high
            txt_both[both + ROWS:both + ROWS + HALF, :] = low

    def sigmoids(row, rows, col, cols):
        def one(at, count):
            a_hi, a_lo = img_hi[rows_at(at, count), :], img_lo[rows_at(at, count), :]
            wide = cols - cols % 256
            if wide:
                b_hi, b_lo = txt_hi[col:col + wide, :], txt_lo[col:col + wide, :]
                dots = dot_nt(a_hi, b_hi) + (dot_nt(a_hi, b_lo) + dot_nt(a_lo, b_hi))
                sig[rows_at(at, count), col:col + wide] = jax.nn.sigmoid(temper * dots + offset)
            if cols % 256:
                last = col + wide
                both = dot_nt(a_hi, txt_both[2 * last:2 * last + 2 * ROWS, :])
                dots = both[:, :ROWS] + (both[:, ROWS:] + dot_nt(a_lo, txt_hi[last:last + ROWS, :]))
                sig[rows_at(at, count), last:last + ROWS] = jax.nn.sigmoid(temper * dots + offset)

        if rows <= 256:
            one(row, rows)
        else:
            def turn(i, carry):
                one(pl.multiple_of(row + i * 256, 256), 256)
                return carry

            lax.fori_loop(0, rows // 256, turn, 0)

    def times(left, high, low, store):
        l_hi, l_lo = split(left)
        for at, count in COLS:
            cs = slice(at, at + count)
            store(cs, dot_nn(l_hi, high[:, cs]) + (dot_nn(l_hi, low[:, cs]) + dot_nn(l_lo, high[:, cs])))

    def image_grads(first, cols=4 * ROWS):
        def store(cs, value):
            g_img[first:first + 2 * ROWS, cs] = value

        times(sig[first:first + 2 * ROWS, 0:cols], txt_hi.at[0:cols], txt_lo.at[0:cols], store)

    def add_image_grads(first, step, rows=ROWS):
        s_hi, s_lo = split(sig[first:first + rows, ROWS * step:ROWS * (step + 1)])
        s_hi = jnp.concatenate([s_hi, s_hi], axis=1)
        for at, count in COLS:
            cs = slice(at, at + count)
            g_img[first:first + rows, cs] += (
                dot_nn(s_hi, txt_both[2 * ROWS * step:2 * ROWS * (step + 1), cs])
                + dot_nn(s_lo, txt_hi[ROWS * step:ROWS * (step + 1), cs])
            )

    def text_grads(first, row=0, rows=8 * ROWS, add=False):
        def store(cs, value):
            g_txt[first:first + ROWS, cs] = g_txt[first:first + ROWS, cs] + value if add else value

        times(sig[row:row + rows, first:first + ROWS].T, img_hi.at[row:row + rows], img_lo.at[row:row + rows], store)

    def add_text_grads(first, row):
        s_hi, s_lo = split(sig[row:row + ROWS, first:first + ROWS].T)
        s_hi = jnp.concatenate([s_hi, s_hi], axis=1)
        for at, count in COLS:
            cs = slice(at, at + count)
            both = jnp.concatenate([img_hi[row:row + ROWS, cs], img_lo[row:row + ROWS, cs]], axis=0)
            g_txt[first:first + ROWS, cs] += dot_nn(s_hi, both) + dot_nn(s_lo, img_hi[row:row + ROWS, cs])

    for axis in ("x", "z"):
        for side in (0, 1):
            gather(axis, 1, side, 0)
    loaded(1)
    normalize(1)
    for axis in ("x", "z"):
        for side in (0, 1):
            gather(axis, 1, side, 1)
    for part in (0, 1):
        for axis in ("x", "z"):
            for side in (0, 1):
                gather(axis, 2, side, part)
    across(0)
    for each in small:
        each.wait()
    meta[0, 0:4, :] = pos_ref[...]
    meta[0, 4:5, :] = cnt_ref[...]
    meta[0, 5:6, :] = row_ref[...]
    meta[0, 6:8, :] = jnp.zeros((2, ROWS), jnp.int32)
    for slot, device in ((1, y_dev[0]), (2, y_dev[1]), (3, y_far)):
        push("m", meta.at[0], meta.at[slot], device, LISTS)
    for step in (1, 2):
        for side in (0, 1):
            gather_y("yt", step, side)

    split_img(0)
    split_txt(0)
    crossed(0)
    split_img(ROWS)
    sigmoids(0, 256, 0, ROWS)

    arrived("m", meta.at[1:4])
    group_base = blk * (4 * ROWS)
    places = [lax.rem(grp + shift, 4) * ROWS + group_base for shift in (0, 3, 1, 2)]
    tall = lax.broadcasted_iota(jnp.int32, (ROWS, ROWS), 0)

    def named(slot):
        tiles = []
        for ids in range(4):
            hit = None
            for k in range(4):
                listed = jnp.where(meta[slot, 4:5, :] > k, meta[slot, k:k + 1, :], -1)
                same = listed == tall + places[ids]
                hit = same if hit is None else hit | same
            tiles.append(jnp.where(hit, 1.0, 0.0).astype(BF16))
        return jnp.concatenate(tiles, axis=0)

    def held(slot):
        tiles = [
            jnp.where(meta[ids, 5:6, :] == tall + places[slot], 1.0, 0.0).astype(BF16)
            for ids in range(4)
        ]
        return jnp.concatenate(tiles, axis=1)

    own_ids, own_held = named(0), held(0)
    mark_a[:, 0:ROWS] = dot_nn(own_held, own_ids)
    for slot in (1, 2, 3):
        mark_a[:, slot * ROWS:(slot + 1) * ROWS] = dot_nn(own_held, named(slot))
        mark_b[(slot - 1) * ROWS:slot * ROWS, :] = dot_nn(held(slot), own_ids)

    for axis in ("x", "z"):
        for side in (0, 1):
            near(axis, side)
            for part in (0, 1):
                gather(axis, 3, side, part)
    across(1)
    forward_y("yt")
    for step in (1, 2):
        for side in (0, 1):
            gather_y("yi", step, side)

    split_txt(1)
    split_img(256)
    sigmoids(0, 256, ROWS, ROWS)
    sigmoids(256, ROWS, 0, 256)
    crossed(1)
    split_img(256 + ROWS)
    sigmoids(256 + ROWS, ROWS, 0, 256)
    image_grads(256, 2 * ROWS)
    text_grads(ROWS, 0, 512)

    near_rest("x")
    across(2)
    near_rest("z")
    split_txt(2)
    split_img(512)
    sigmoids(0, 512, 2 * ROWS, ROWS)
    add_image_grads(256, 2, 2 * ROWS)
    sigmoids(512, ROWS, 0, 3 * ROWS)
    add_text_grads(ROWS, 512)
    crossed(2)
    split_img(512 + ROWS)
    sigmoids(512 + ROWS, ROWS, 0, 3 * ROWS)
    add_text_grads(ROWS, 512 + ROWS)

    far("x", 0)
    across_far(0)
    far("z", 0)
    split_txt(3, 0, HALF)
    split_img(768, HALF)
    far("x", 1)
    across_far(1)
    far("z", 1)

    def share(step):
        first = 2 * ROWS * step
        push(("r", step), g_img.at[rows_at(first + ROWS, ROWS)], c_in.at[step], peer, CORE)

    def joined(step):
        first = 2 * ROWS * step
        arrived(("r", step), c_in.at[step])
        g_img[first:first + ROWS, :] += c_in[step]

    def share_far(part):
        first = 6 * ROWS + part * ROWS + HALF
        push(("r", 3), g_img.at[rows_at(first, HALF)], c_in.at[3, rows_at(part * HALF, HALF)], peer, CORE)

    def joined_far():
        arrived(("r", 3), c_in.at[3])
        for part in (0, 1):
            first = 6 * ROWS + part * ROWS
            g_img[first:first + HALF, :] += c_in[3, part * HALF:(part + 1) * HALF]

    scatters = {"x": (g_img, 2 * ROWS, x_dev, x_in, x_far), "z": (g_txt, ROWS, z_dev, z_in, z_far)}

    def scatter_near(axis):
        buffer, stride, devices, inbox, _ = scatters[axis]
        for side in (0, 1):
            first = stride + (1 - side) * HALF
            push((axis, "s", 1), buffer.at[rows_at(first, HALF)], inbox.at[0, side], devices[side], SCATTER)

    def scatter_far(axis):
        buffer, stride, devices, _, inbox = scatters[axis]
        for part in (0, 1):
            for side in (0, 1):
                first = place_of(axis, 3, side, part)
                push((axis, "s", 3, part), buffer.at[rows_at(first, PIECE)], inbox.at[part, side], devices[side], SCATTER)

    def scatter_rest(axis, part):
        buffer, stride, devices, inbox, relay = scatters[axis]
        arrived((axis, "s", 3, part), relay.at[part])
        for side in (0, 1):
            first = 2 * stride + (1 - side) * HALF + part * PIECE
            buffer[first:first + PIECE, :] += relay[part, side]
            push(
                (axis, "s", 2, part), buffer.at[rows_at(first, PIECE)], inbox.at[1 + part, side, rows_at(0, PIECE)],
                devices[side], SCATTER,
            )

    split_txt(3, HALF, HALF)
    sigmoids(256, 256, 3 * ROWS, ROWS)
    add_image_grads(256 + ROWS, 3)
    share(1)
    add_image_grads(256, 3)
    split_img(896, HALF)
    crossed_far(0)
    split_img(768 + HALF, HALF)
    sigmoids(768, ROWS, ROWS, ROWS)
    add_text_grads(ROWS, 768)
    crossed_far(1)
    split_img(896 + HALF, HALF)
    sigmoids(896, ROWS, ROWS, ROWS)
    add_text_grads(ROWS, 896)
    scatter_near("z")
    joined(1)
    scatter_near("x")

    sigmoids(768, 256, 0, ROWS)
    sigmoids(768, 256, 2 * ROWS, 2 * ROWS)
    image_grads(768)
    share_far(0)
    share_far(1)
    sigmoids(0, 256, 3 * ROWS, ROWS)
    sigmoids(512, 256, 3 * ROWS, ROWS)
    text_grads(3 * ROWS)
    scatter_far("z")
    joined_far()
    scatter_far("x")

    forward_y("yi")

    image_grads(512)
    share(2)
    text_grads(2 * ROWS)
    joined(2)

    sig[0:ROWS, 0:ROWS] -= mark_a[:, 0:ROWS]
    image_grads(0)
    share(0)
    text_grads(0)
    scatter_rest("x", 0)
    scatter_rest("z", 0)

    arrived(("yt", 2), y_txt.at[ROWS:3 * ROWS])
    split_rows(y_txt, yt_hi, yt_lo, 0, 3 * ROWS)
    own = rows_at(0, ROWS)
    dots = dot_nt(img_hi[own, :], yt_hi[...]) + (dot_nt(img_hi[own, :], yt_lo[...]) + dot_nt(img_lo[own, :], yt_hi[...]))
    coef = mark_a[:, ROWS:4 * ROWS] * (jax.nn.sigmoid(temper * dots + offset) - 1.0)

    def add_img(cs, value):
        g_img[0:ROWS, cs] += value

    times(coef, yt_hi, yt_lo, add_img)
    scatter_rest("x", 1)
    scatter_rest("z", 1)
    joined(0)

    arrived(("yi", 2), y_img.at[ROWS:3 * ROWS])
    split_rows(y_img, yi_hi, yi_lo, 0, 3 * ROWS)
    dots = dot_nt(yi_hi[...], txt_hi[own, :]) + (dot_nt(yi_hi[...], txt_lo[own, :]) + dot_nt(yi_lo[...], txt_hi[own, :]))
    coef = mark_b[...] * (jax.nn.sigmoid(temper * dots + offset) - 1.0)

    def add_txt(cs, value):
        g_txt[0:ROWS, cs] += value

    times(coef.T, yi_hi, yi_lo, add_txt)

    ends = (
        ("x", g_img, x_in, img, norm_img, gimg_ref),
        ("z", g_txt, z_in, txt, norm_txt, gtxt_ref),
    )
    for axis, sums, inbox, unit, norm, out in ends:
        arrived((axis, "s", 1), inbox.at[0])
        for side in (0, 1):
            at = slice((1 - side) * HALF, (2 - side) * HALF)
            sums[at, :] += inbox[0, side]
    for part in (0, 1):
        for axis, sums, inbox, unit, norm, out in ends:
            arrived((axis, "s", 2, part), inbox.at[1 + part, :, rows_at(0, PIECE)])
            for half in (0, 1):
                at = slice(half * HALF + part * PIECE, half * HALF + (part + 1) * PIECE)
                grad = temper * (sums[at, :] + inbox[1 + part, half, 0:PIECE])
                units = unit[at, :]
                along = jnp.sum(units * grad, axis=1, keepdims=True)
                out[at, :] = (grad - units * along) / norm[at, :]

    done(send_sem.at[CORE], g_img)
    done(send_sem.at[GATHER], g_img.at[0:6 * ROWS])
    done(send_sem.at[ALONG_Y], g_img.at[0:6 * ROWS])
    done(send_sem.at[SCATTER], g_img.at[0:6 * ROWS])
    done(send_sem.at[LISTS], meta.at[1:4])


def hand_on(gimg_in, gtxt_in, gimg_out, gtxt_out, sems):
    copies = [
        pltpu.make_async_copy(gimg_in, gimg_out, sems.at[0]),
        pltpu.make_async_copy(gtxt_in, gtxt_out, sems.at[1]),
    ]
    for copy in copies:
        copy.start()
    for copy in copies:
        copy.wait()


def body(image_emb, text_emb, logit_scale, logit_bias, pos_image, pos_count, image_row):
    anywhere = pl.BlockSpec(memory_space=pl.ANY)
    vmem = pl.BlockSpec(memory_space=pltpu.VMEM)
    rows = jax.ShapeDtypeStruct((ROWS, D), F32)
    grads = pl.pallas_call(
        kernel,
        out_shape=(pltpu.VMEM((ROWS, D), F32), pltpu.VMEM((ROWS, D), F32)),
        in_specs=[pl.BlockSpec(memory_space=pltpu.SMEM)] * 2 + [pl.BlockSpec(memory_space=pltpu.HBM)] * 5,
        out_specs=(vmem, vmem),
        scratch_shapes=[
            pltpu.VMEM((ROWS, D), F32),
            pltpu.VMEM((ROWS, D), F32),
            pltpu.VMEM((4, ROWS), jnp.int32),
            pltpu.VMEM((1, ROWS), jnp.int32),
            pltpu.VMEM((1, ROWS), jnp.int32),
            pltpu.SemaphoreType.DMA((5,)),
            pltpu.VMEM((8 * ROWS, D), F32),
            pltpu.VMEM((4 * ROWS, D), F32),
            pltpu.VMEM((8 * ROWS, D), BF16),
            pltpu.VMEM((8 * ROWS, D), BF16),
            pltpu.VMEM((4 * ROWS, D), BF16),
            pltpu.VMEM((4 * ROWS, D), BF16),
            pltpu.VMEM((8 * ROWS, 4 * ROWS), F32),
            pltpu.VMEM((8 * ROWS, D), F32),
            pltpu.VMEM((4 * ROWS, D), F32),
            pltpu.VMEM((3 * ROWS, D), F32),
            pltpu.VMEM((3 * ROWS, D), F32),
            pltpu.VMEM((3 * ROWS, D), BF16),
            pltpu.VMEM((3 * ROWS, D), BF16),
            pltpu.VMEM((3 * ROWS, D), BF16),
            pltpu.VMEM((3 * ROWS, D), BF16),
            pltpu.VMEM((8 * ROWS, D), BF16),
            pltpu.VMEM((3, 2, HALF, D), F32),
            pltpu.VMEM((3, 2, HALF, D), F32),
            pltpu.VMEM((2, 2, PIECE, D), F32),
            pltpu.VMEM((2, 2, PIECE, D), F32),
            pltpu.VMEM((4, ROWS, D), F32),
            pltpu.VMEM((4, 8, ROWS), jnp.int32),
            pltpu.VMEM((ROWS, 4 * ROWS), F32),
            pltpu.VMEM((3 * ROWS, ROWS), F32),
            pltpu.VMEM((ROWS, 1), F32),
            pltpu.VMEM((ROWS, 1), F32),
            pltpu.SemaphoreType.DMA((N_SEND,)),
            pltpu.SemaphoreType.DMA((N_RECV,)),
        ],
        compiler_params=pltpu.CompilerParams(
            collective_id=0, has_side_effects=True, vmem_limit_bytes=46 * 2**20
        ),
        name="align_step",
    )(
        logit_scale,
        logit_bias,
        *(
            pltpu.with_memory_space_constraint(operand, pltpu.HBM)
            for operand in (
                image_emb, text_emb, pos_image.T, pos_count.reshape(1, ROWS), image_row.reshape(1, ROWS),
            )
        ),
    )
    grads = [pltpu.with_memory_space_constraint(grad, pltpu.VMEM) for grad in grads]
    return pl.pallas_call(
        hand_on,
        out_shape=(rows, rows),
        in_specs=[anywhere, anywhere],
        out_specs=(anywhere, anywhere),
        scratch_shapes=[pltpu.SemaphoreType.DMA((2,))],
        name="hand_on",
    )(*grads)


def solution(mesh):
    return jax.shard_map(
        body,
        mesh=mesh,
        in_specs=(
            P(("blk", "grp"), None),
            P(("blk", "grp"), None),
            P(),
            P(),
            P(("blk", "grp"), None),
            P(("blk", "grp")),
            P(("blk", "grp")),
        ),
        out_specs=(P(("blk", "grp"), None), P(("blk", "grp"), None)),
        check_vma=False,
    )
```

```python
import functools

import jax
import jax.numpy as jnp
from jax import lax
from jax.experimental import pallas as pl
from jax.experimental.pallas import tpu as pltpu
from jax.sharding import PartitionSpec as P

ROWS = 128
HALF = 64
PIECE = 32
D = 1152
COLS = ((0, 256), (256, 256), (512, 256), (768, 256), (1024, 128))
N_SEND = 5
N_RECV = 36
CORE, GATHER, ALONG_Y, SCATTER, LISTS = range(N_SEND)
F32 = jnp.float32
BF16 = jnp.bfloat16


def rows_at(start, count):
    return pl.ds(start, count)


def split(values):
    high = values.astype(BF16)
    return high, (values - high.astype(F32)).astype(BF16)


def dot_nn(a, b):
    return lax.dot_general(a, b, (((1,), (0,)), ((), ())), preferred_element_type=F32)


def dot_nt(a, b):
    return lax.dot_general(a, b, (((1,), (1,)), ((), ())), preferred_element_type=F32)


def kernel(
    scale_ref, bias_ref, img_hbm, txt_hbm, pos_hbm, cnt_hbm, row_hbm,
    gimg_ref, gtxt_ref,
    img_ref, txt_ref, pos_ref, cnt_ref, row_ref, load_sem,
    img, txt, img_hi, img_lo, txt_hi, txt_lo, sig, g_img, g_txt,
    y_txt, y_img, yt_hi, yt_lo, yi_hi, yi_lo,
    txt_both, x_in, z_in, x_far, z_far, c_in, meta, mark_a, mark_b, norm_img, norm_txt, send_sem, recv_sem,
):
    blk, grp = lax.axis_index("blk"), lax.axis_index("grp")
    core = lax.rem(blk, 2)
    x = lax.rem(lax.div(blk, 2), 4)
    z = lax.div(blk, 8)

    def place(dz, dx, dg):
        zz, xx, gg = lax.rem(z + dz, 4), lax.rem(x + dx, 4), lax.rem(grp + dg, 4)
        return ((zz * 4 + xx) * 2 + core, gg)

    x_dev = (place(0, 1, 0), place(0, 3, 0))
    z_dev = (place(1, 0, 0), place(3, 0, 0))
    y_dev = (place(0, 0, 1), place(0, 0, 3))
    y_far = place(0, 0, 2)
    peer = ((z * 4 + x) * 2 + 1 - core, grp)
    partners = x_dev + z_dev + y_dev + (y_far, peer)

    barrier = pltpu.get_barrier_semaphore()
    for other in partners:
        pl.semaphore_signal(barrier, inc=1, device_id=other, device_id_type=pl.DeviceIdType.MESH)

    temper = scale_ref[0]
    offset = bias_ref[0]
    sources = ((img_hbm, img_ref, img, norm_img), (txt_hbm, txt_ref, txt, norm_txt))

    def load(part):
        for hbm, ref, _, _ in sources:
            for half in (0, 1):
                at = rows_at(half * HALF + part * PIECE, PIECE)
                pltpu.make_async_copy(hbm.at[at], ref.at[at], load_sem.at[part]).start()

    def loaded(part):
        pltpu.make_async_copy(img_hbm, img_ref, load_sem.at[part]).wait()

    load(0)
    small = [
        pltpu.make_async_copy(source, target, load_sem.at[2 + at])
        for at, (source, target) in enumerate(((pos_hbm, pos_ref), (cnt_hbm, cnt_ref), (row_hbm, row_ref)))
    ]
    for each in small:
        each.start()

    def normalize(part):
        for _, ref, unit, norm in sources:
            for half in (0, 1):
                at = rows_at(half * HALF + part * PIECE, PIECE)
                values = ref[at, :]
                length = jnp.sqrt(jnp.sum(values * values, axis=1, keepdims=True) + 1e-06)
                norm[at, :] = length
                unit[at, :] = values / length

    loaded(0)
    load(1)
    normalize(0)
    pl.semaphore_wait(barrier, len(partners))

    groups = {}

    def push(group, source, target, device, send):
        at = groups.setdefault(group, len(groups))
        pltpu.make_async_remote_copy(
            src_ref=source, dst_ref=target, send_sem=send_sem.at[send], recv_sem=recv_sem.at[at],
            device_id=device, device_id_type=pl.DeviceIdType.MESH,
        ).start()

    def done(sem, region):
        pltpu.make_async_copy(region, region, sem).wait()

    def arrived(group, region):
        done(recv_sem.at[groups[group]], region)

    rings = {"x": (img, 2 * ROWS, x_dev), "z": (txt, ROWS, z_dev)}

    def place_of(axis, step, side, part):
        stride = rings[axis][1]
        if step == 3:
            return 3 * stride + part * (stride // 2) + side * PIECE
        return stride * step + side * HALF + part * PIECE

    def gather(axis, step, side, part):
        buffer, stride, devices = rings[axis]
        first = {1: side * HALF, 2: (1 - side) * HALF, 3: stride + side * HALF}[step]
        push(
            {1: (axis, 1, side), 2: (axis, 2), 3: (axis, 3, part)}[step],
            buffer.at[rows_at(first + part * PIECE, PIECE)],
            buffer.at[rows_at(place_of(axis, step, side, part), PIECE)],
            devices[side],
            GATHER,
        )

    def near(axis, side):
        buffer, stride, _ = rings[axis]
        arrived((axis, 1, side), buffer.at[rows_at(stride + side * HALF, HALF)])

    def near_rest(axis):
        buffer, stride, _ = rings[axis]
        arrived((axis, 2), buffer.at[rows_at(2 * stride, ROWS)])

    def far(axis, part):
        buffer, stride, _ = rings[axis]
        arrived((axis, 3, part), buffer.at[rows_at(3 * stride + part * (stride // 2), HALF)])

    y_rings = {"yt": (txt, y_txt), "yi": (img, y_img)}

    def gather_y(axis, step, side):
        own, others = y_rings[axis]
        half = side if step != 2 else 1 - side
        if step == 3:
            source = others.at[rows_at(side * ROWS + side * HALF, HALF)]
            target = others.at[rows_at(2 * ROWS + side * HALF, HALF)]
        else:
            source = own.at[rows_at(half * HALF, HALF)]
            target = others.at[rows_at(side * ROWS + half * HALF, HALF)]
        push((axis, 1, side) if step == 1 else (axis, 2), source, target, y_dev[side], ALONG_Y)

    def forward_y(axis):
        others = y_rings[axis][1]
        for side in (0, 1):
            arrived((axis, 1, side), others.at[rows_at(side * ROWS + side * HALF, HALF)])
            gather_y(axis, 3, side)

    def across(step):
        first = 2 * ROWS * step
        push(("c", step), img.at[rows_at(first, ROWS)], img.at[rows_at(first + ROWS, ROWS)], peer, CORE)

    def crossed(step):
        arrived(("c", step), img.at[rows_at(2 * ROWS * step + ROWS, ROWS)])

    def across_far(part):
        first = 6 * ROWS + part * ROWS
        push(("c", 3, part), img.at[rows_at(first, HALF)], img.at[rows_at(first + HALF, HALF)], peer, CORE)

    def crossed_far(part):
        arrived(("c", 3, part), img.at[rows_at(6 * ROWS + part * ROWS + HALF, HALF)])

    def split_rows(source, high, low, first, count):
        for at in range(first, first + count, HALF):
            high[at:at + HALF, :], low[at:at + HALF, :] = split(source[at:at + HALF, :])

    def split_img(first, count=ROWS):
        split_rows(img, img_hi, img_lo, first, count)

    def split_txt(step, first=0, count=ROWS):
        for at in range(ROWS * step + first, ROWS * step + first + count, HALF):
            high, low = split(txt[at:at + HALF, :])
            txt_hi[at:at + HALF, :] = high
            txt_lo[at:at + HALF, :] = low
            both = at + ROWS * step
            txt_both[both:both + HALF, :] = high
            txt_both[both + ROWS:both + ROWS + HALF, :] = low

    def sigmoids(row, rows, col, cols):
        def one(at, count):
            a_hi, a_lo = img_hi[rows_at(at, count), :], img_lo[rows_at(at, count), :]
            wide = cols - cols % 256
            if wide:
                b_hi, b_lo = txt_hi[col:col + wide, :], txt_lo[col:col + wide, :]
                dots = dot_nt(a_hi, b_hi) + (dot_nt(a_hi, b_lo) + dot_nt(a_lo, b_hi))
                sig[rows_at(at, count), col:col + wide] = jax.nn.sigmoid(temper * dots + offset)
            if cols % 256:
                last = col + wide
                both = dot_nt(a_hi, txt_both[2 * last:2 * last + 2 * ROWS, :])
                dots = both[:, :ROWS] + (both[:, ROWS:] + dot_nt(a_lo, txt_hi[last:last + ROWS, :]))
                sig[rows_at(at, count), last:last + ROWS] = jax.nn.sigmoid(temper * dots + offset)

        if rows <= 256:
            one(row, rows)
        else:
            def turn(i, carry):
                one(pl.multiple_of(row + i * 256, 256), 256)
                return carry

            lax.fori_loop(0, rows // 256, turn, 0)

    def times(left, high, low, store):
        l_hi, l_lo = split(left)
        for at, count in COLS:
            cs = slice(at, at + count)
            store(cs, dot_nn(l_hi, high[:, cs]) + (dot_nn(l_hi, low[:, cs]) + dot_nn(l_lo, high[:, cs])))

    def image_grads(first, cols=4 * ROWS):
        def store(cs, value):
            g_img[first:first + 2 * ROWS, cs] = value

        times(sig[first:first + 2 * ROWS, 0:cols], txt_hi.at[0:cols], txt_lo.at[0:cols], store)

    def add_image_grads(first, step, rows=ROWS):
        s_hi, s_lo = split(sig[first:first + rows, ROWS * step:ROWS * (step + 1)])
        s_hi = jnp.concatenate([s_hi, s_hi], axis=1)
        for at, count in COLS:
            cs = slice(at, at + count)
            g_img[first:first + rows, cs] += (
                dot_nn(s_hi, txt_both[2 * ROWS * step:2 * ROWS * (step + 1), cs])
                + dot_nn(s_lo, txt_hi[ROWS * step:ROWS * (step + 1), cs])
            )

    def text_grads(first, row=0, rows=8 * ROWS, add=False):
        def store(cs, value):
            g_txt[first:first + ROWS, cs] = g_txt[first:first + ROWS, cs] + value if add else value

        times(sig[row:row + rows, first:first + ROWS].T, img_hi.at[row:row + rows], img_lo.at[row:row + rows], store)

    def add_text_grads(first, row):
        s_hi, s_lo = split(sig[row:row + ROWS, first:first + ROWS].T)
        s_hi = jnp.concatenate([s_hi, s_hi], axis=1)
        for at, count in COLS:
            cs = slice(at, at + count)
            both = jnp.concatenate([img_hi[row:row + ROWS, cs], img_lo[row:row + ROWS, cs]], axis=0)
            g_txt[first:first + ROWS, cs] += dot_nn(s_hi, both) + dot_nn(s_lo, img_hi[row:row + ROWS, cs])

    for axis in ("x", "z"):
        for side in (0, 1):
            gather(axis, 1, side, 0)
    loaded(1)
    normalize(1)
    for axis in ("x", "z"):
        for side in (0, 1):
            gather(axis, 1, side, 1)
    for part in (0, 1):
        for axis in ("x", "z"):
            for side in (0, 1):
                gather(axis, 2, side, part)
    across(0)
    for each in small:
        each.wait()
    meta[0, 0:4, :] = pos_ref[...]
    meta[0, 4:5, :] = cnt_ref[...]
    meta[0, 5:6, :] = row_ref[...]
    meta[0, 6:8, :] = jnp.zeros((2, ROWS), jnp.int32)
    for slot, device in ((1, y_dev[0]), (2, y_dev[1]), (3, y_far)):
        push("m", meta.at[0], meta.at[slot], device, LISTS)
    for step in (1, 2):
        for side in (0, 1):
            gather_y("yt", step, side)

    split_img(0)
    split_txt(0)
    crossed(0)
    split_img(ROWS)
    sigmoids(0, 256, 0, ROWS)

    arrived("m", meta.at[1:4])
    group_base = blk * (4 * ROWS)
    places = [lax.rem(grp + shift, 4) * ROWS + group_base for shift in (0, 3, 1, 2)]
    tall = lax.broadcasted_iota(jnp.int32, (ROWS, ROWS), 0)

    def named(slot):
        tiles = []
        for ids in range(4):
            hit = None
            for k in range(4):
                listed = jnp.where(meta[slot, 4:5, :] > k, meta[slot, k:k + 1, :], -1)
                same = listed == tall + places[ids]
                hit = same if hit is None else hit | same
            tiles.append(jnp.where(hit, 1.0, 0.0).astype(BF16))
        return jnp.concatenate(tiles, axis=0)

    def held(slot):
        tiles = [
            jnp.where(meta[ids, 5:6, :] == tall + places[slot], 1.0, 0.0).astype(BF16)
            for ids in range(4)
        ]
        return jnp.concatenate(tiles, axis=1)

    own_ids, own_held = named(0), held(0)
    mark_a[:, 0:ROWS] = dot_nn(own_held, own_ids)
    for slot in (1, 2, 3):
        mark_a[:, slot * ROWS:(slot + 1) * ROWS] = dot_nn(own_held, named(slot))
        mark_b[(slot - 1) * ROWS:slot * ROWS, :] = dot_nn(held(slot), own_ids)

    for axis in ("x", "z"):
        for side in (0, 1):
            near(axis, side)
            for part in (0, 1):
                gather(axis, 3, side, part)
    across(1)
    forward_y("yt")
    for step in (1, 2):
        for side in (0, 1):
            gather_y("yi", step, side)

    split_txt(1)
    split_img(256)
    sigmoids(0, 256, ROWS, ROWS)
    sigmoids(256, ROWS, 0, 256)
    crossed(1)
    split_img(256 + ROWS)
    sigmoids(256 + ROWS, ROWS, 0, 256)
    image_grads(256, 2 * ROWS)
    text_grads(ROWS, 0, 512)

    near_rest("x")
    across(2)
    near_rest("z")
    split_txt(2)
    split_img(512)
    sigmoids(0, 512, 2 * ROWS, ROWS)
    add_image_grads(256, 2, 2 * ROWS)
    sigmoids(512, ROWS, 0, 3 * ROWS)
    add_text_grads(ROWS, 512)
    crossed(2)
    split_img(512 + ROWS)
    sigmoids(512 + ROWS, ROWS, 0, 3 * ROWS)
    add_text_grads(ROWS, 512 + ROWS)

    far("x", 0)
    across_far(0)
    far("z", 0)
    split_txt(3, 0, HALF)
    split_img(768, HALF)
    far("x", 1)
    across_far(1)
    far("z", 1)

    def share(step):
        first = 2 * ROWS * step
        push(("r", step), g_img.at[rows_at(first + ROWS, ROWS)], c_in.at[step], peer, CORE)

    def joined(step):
        first = 2 * ROWS * step
        arrived(("r", step), c_in.at[step])
        g_img[first:first + ROWS, :] += c_in[step]

    def share_far(part):
        first = 6 * ROWS + part * ROWS + HALF
        push(("r", 3), g_img.at[rows_at(first, HALF)], c_in.at[3, rows_at(part * HALF, HALF)], peer, CORE)

    def joined_far():
        arrived(("r", 3), c_in.at[3])
        for part in (0, 1):
            first = 6 * ROWS + part * ROWS
            g_img[first:first + HALF, :] += c_in[3, part * HALF:(part + 1) * HALF]

    scatters = {"x": (g_img, 2 * ROWS, x_dev, x_in, x_far), "z": (g_txt, ROWS, z_dev, z_in, z_far)}

    def scatter_near(axis):
        buffer, stride, devices, inbox, _ = scatters[axis]
        for side in (0, 1):
            first = stride + (1 - side) * HALF
            push((axis, "s", 1), buffer.at[rows_at(first, HALF)], inbox.at[0, side], devices[side], SCATTER)

    def scatter_far(axis):
        buffer, stride, devices, _, inbox = scatters[axis]
        for part in (0, 1):
            for side in (0, 1):
                first = place_of(axis, 3, side, part)
                push((axis, "s", 3, part), buffer.at[rows_at(first, PIECE)], inbox.at[part, side], devices[side], SCATTER)

    def scatter_rest(axis, part):
        buffer, stride, devices, inbox, relay = scatters[axis]
        arrived((axis, "s", 3, part), relay.at[part])
        for side in (0, 1):
            first = 2 * stride + (1 - side) * HALF + part * PIECE
            buffer[first:first + PIECE, :] += relay[part, side]
            push(
                (axis, "s", 2, part), buffer.at[rows_at(first, PIECE)], inbox.at[1 + part, side, rows_at(0, PIECE)],
                devices[side], SCATTER,
            )

    split_txt(3, HALF, HALF)
    sigmoids(256, 256, 3 * ROWS, ROWS)
    add_image_grads(256 + ROWS, 3)
    share(1)
    add_image_grads(256, 3)

    @pl.when(core == 0)
    def _():
        joined(1)
        scatter_near("x")

    split_img(896, HALF)
    crossed_far(0)
    split_img(768 + HALF, HALF)
    sigmoids(768, ROWS, ROWS, ROWS)
    add_text_grads(ROWS, 768)
    crossed_far(1)
    split_img(896 + HALF, HALF)
    sigmoids(896, ROWS, ROWS, ROWS)
    add_text_grads(ROWS, 896)
    scatter_near("z")
    @pl.when(core == 1)
    def _():
        joined(1)
        scatter_near("x")

    sigmoids(768, 256, 0, ROWS)
    sigmoids(768, 256, 2 * ROWS, 2 * ROWS)
    image_grads(768)
    share_far(0)
    share_far(1)
    sigmoids(0, 256, 3 * ROWS, ROWS)
    sigmoids(512, 256, 3 * ROWS, ROWS)
    text_grads(3 * ROWS)
    scatter_far("z")
    joined_far()
    scatter_far("x")

    forward_y("yi")

    image_grads(512)
    share(2)
    text_grads(2 * ROWS)
    joined(2)

    sig[0:ROWS, 0:ROWS] -= mark_a[:, 0:ROWS]
    image_grads(0)
    share(0)
    text_grads(0)
    scatter_rest("x", 0)
    scatter_rest("z", 0)

    arrived(("yt", 2), y_txt.at[ROWS:3 * ROWS])
    split_rows(y_txt, yt_hi, yt_lo, 0, 3 * ROWS)
    own = rows_at(0, ROWS)
    dots = dot_nt(img_hi[own, :], yt_hi[...]) + (dot_nt(img_hi[own, :], yt_lo[...]) + dot_nt(img_lo[own, :], yt_hi[...]))
    coef = mark_a[:, ROWS:4 * ROWS] * (jax.nn.sigmoid(temper * dots + offset) - 1.0)

    def add_img(cs, value):
        g_img[0:ROWS, cs] += value

    times(coef, yt_hi, yt_lo, add_img)
    scatter_rest("x", 1)
    scatter_rest("z", 1)
    joined(0)

    arrived(("yi", 2), y_img.at[ROWS:3 * ROWS])
    split_rows(y_img, yi_hi, yi_lo, 0, 3 * ROWS)
    dots = dot_nt(yi_hi[...], txt_hi[own, :]) + (dot_nt(yi_hi[...], txt_lo[own, :]) + dot_nt(yi_lo[...], txt_hi[own, :]))
    coef = mark_b[...] * (jax.nn.sigmoid(temper * dots + offset) - 1.0)

    def add_txt(cs, value):
        g_txt[0:ROWS, cs] += value

    times(coef.T, yi_hi, yi_lo, add_txt)

    ends = (
        ("x", g_img, x_in, img, norm_img, gimg_ref),
        ("z", g_txt, z_in, txt, norm_txt, gtxt_ref),
    )
    for axis, sums, inbox, unit, norm, out in ends:
        arrived((axis, "s", 1), inbox.at[0])
        for side in (0, 1):
            at = slice((1 - side) * HALF, (2 - side) * HALF)
            sums[at, :] += inbox[0, side]
    for part in (0, 1):
        for axis, sums, inbox, unit, norm, out in ends:
            arrived((axis, "s", 2, part), inbox.at[1 + part, :, rows_at(0, PIECE)])
            for half in (0, 1):
                at = slice(half * HALF + part * PIECE, half * HALF + (part + 1) * PIECE)
                grad = temper * (sums[at, :] + inbox[1 + part, half, 0:PIECE])
                units = unit[at, :]
                along = jnp.sum(units * grad, axis=1, keepdims=True)
                out[at, :] = (grad - units * along) / norm[at, :]

    done(send_sem.at[CORE], g_img)
    done(send_sem.at[GATHER], g_img.at[0:6 * ROWS])
    done(send_sem.at[ALONG_Y], g_img.at[0:6 * ROWS])
    done(send_sem.at[SCATTER], g_img.at[0:6 * ROWS])
    done(send_sem.at[LISTS], meta.at[1:4])


def hand_on(gimg_in, gtxt_in, gimg_out, gtxt_out, sems):
    copies = [
        pltpu.make_async_copy(gimg_in, gimg_out, sems.at[0]),
        pltpu.make_async_copy(gtxt_in, gtxt_out, sems.at[1]),
    ]
    for copy in copies:
        copy.start()
    for copy in copies:
        copy.wait()


def body(image_emb, text_emb, logit_scale, logit_bias, pos_image, pos_count, image_row):
    anywhere = pl.BlockSpec(memory_space=pl.ANY)
    vmem = pl.BlockSpec(memory_space=pltpu.VMEM)
    rows = jax.ShapeDtypeStruct((ROWS, D), F32)
    grads = pl.pallas_call(
        kernel,
        out_shape=(pltpu.VMEM((ROWS, D), F32), pltpu.VMEM((ROWS, D), F32)),
        in_specs=[pl.BlockSpec(memory_space=pltpu.SMEM)] * 2 + [pl.BlockSpec(memory_space=pltpu.HBM)] * 5,
        out_specs=(vmem, vmem),
        scratch_shapes=[
            pltpu.VMEM((ROWS, D), F32),
            pltpu.VMEM((ROWS, D), F32),
            pltpu.VMEM((4, ROWS), jnp.int32),
            pltpu.VMEM((1, ROWS), jnp.int32),
            pltpu.VMEM((1, ROWS), jnp.int32),
            pltpu.SemaphoreType.DMA((5,)),
            pltpu.VMEM((8 * ROWS, D), F32),
            pltpu.VMEM((4 * ROWS, D), F32),
            pltpu.VMEM((8 * ROWS, D), BF16),
            pltpu.VMEM((8 * ROWS, D), BF16),
            pltpu.VMEM((4 * ROWS, D), BF16),
            pltpu.VMEM((4 * ROWS, D), BF16),
            pltpu.VMEM((8 * ROWS, 4 * ROWS), F32),
            pltpu.VMEM((8 * ROWS, D), F32),
            pltpu.VMEM((4 * ROWS, D), F32),
            pltpu.VMEM((3 * ROWS, D), F32),
            pltpu.VMEM((3 * ROWS, D), F32),
            pltpu.VMEM((3 * ROWS, D), BF16),
            pltpu.VMEM((3 * ROWS, D), BF16),
            pltpu.VMEM((3 * ROWS, D), BF16),
            pltpu.VMEM((3 * ROWS, D), BF16),
            pltpu.VMEM((8 * ROWS, D), BF16),
            pltpu.VMEM((3, 2, HALF, D), F32),
            pltpu.VMEM((3, 2, HALF, D), F32),
            pltpu.VMEM((2, 2, PIECE, D), F32),
            pltpu.VMEM((2, 2, PIECE, D), F32),
            pltpu.VMEM((4, ROWS, D), F32),
            pltpu.VMEM((4, 8, ROWS), jnp.int32),
            pltpu.VMEM((ROWS, 4 * ROWS), F32),
            pltpu.VMEM((3 * ROWS, ROWS), F32),
            pltpu.VMEM((ROWS, 1), F32),
            pltpu.VMEM((ROWS, 1), F32),
            pltpu.SemaphoreType.DMA((N_SEND,)),
            pltpu.SemaphoreType.DMA((N_RECV,)),
        ],
        compiler_params=pltpu.CompilerParams(
            collective_id=0, has_side_effects=True, vmem_limit_bytes=46 * 2**20
        ),
        name="align_step",
    )(
        logit_scale,
        logit_bias,
        *(
            pltpu.with_memory_space_constraint(operand, pltpu.HBM)
            for operand in (
                image_emb, text_emb, pos_image.T, pos_count.reshape(1, ROWS), image_row.reshape(1, ROWS),
            )
        ),
    )
    grads = [pltpu.with_memory_space_constraint(grad, pltpu.VMEM) for grad in grads]
    return pl.pallas_call(
        hand_on,
        out_shape=(rows, rows),
        in_specs=[anywhere, anywhere],
        out_specs=(anywhere, anywhere),
        scratch_shapes=[pltpu.SemaphoreType.DMA((2,))],
        name="hand_on",
    )(*grads)


def solution(mesh):
    return jax.shard_map(
        body,
        mesh=mesh,
        in_specs=(
            P(("blk", "grp"), None),
            P(("blk", "grp"), None),
            P(),
            P(),
            P(("blk", "grp"), None),
            P(("blk", "grp")),
            P(("blk", "grp")),
        ),
        out_specs=(P(("blk", "grp"), None), P(("blk", "grp"), None)),
        check_vma=False,
    )
```

```python
import functools

import jax
import jax.numpy as jnp
from jax import lax
from jax.experimental import pallas as pl
from jax.experimental.pallas import tpu as pltpu
from jax.sharding import PartitionSpec as P

ROWS = 128
HALF = 64
PIECE = 32
D = 1152
COLS = ((0, 256), (256, 256), (512, 256), (768, 256), (1024, 128))
N_SEND = 5
N_RECV = 36
CORE, GATHER, ALONG_Y, SCATTER, LISTS = range(N_SEND)
F32 = jnp.float32
BF16 = jnp.bfloat16


def rows_at(start, count):
    return pl.ds(start, count)


def split(values):
    high = values.astype(BF16)
    return high, (values - high.astype(F32)).astype(BF16)


def dot_nn(a, b):
    return lax.dot_general(a, b, (((1,), (0,)), ((), ())), preferred_element_type=F32)


def dot_nt(a, b):
    return lax.dot_general(a, b, (((1,), (1,)), ((), ())), preferred_element_type=F32)


def kernel(
    scale_ref, bias_ref, img_hbm, txt_hbm, pos_hbm, cnt_hbm, row_hbm,
    gimg_ref, gtxt_ref,
    img_ref, txt_ref, pos_ref, cnt_ref, row_ref, load_sem,
    img, txt, img_hi, img_lo, txt_hi, txt_lo, sig, g_img, g_txt,
    y_txt, y_img, yt_hi, yt_lo, yi_hi, yi_lo,
    txt_both, x_in, z_in, x_far, z_far, c_in, meta, mark_a, mark_b, norm_img, norm_txt, send_sem, recv_sem,
):
    blk, grp = lax.axis_index("blk"), lax.axis_index("grp")
    core = lax.rem(blk, 2)
    x = lax.rem(lax.div(blk, 2), 4)
    z = lax.div(blk, 8)

    def place(dz, dx, dg):
        zz, xx, gg = lax.rem(z + dz, 4), lax.rem(x + dx, 4), lax.rem(grp + dg, 4)
        return ((zz * 4 + xx) * 2 + core, gg)

    x_dev = (place(0, 1, 0), place(0, 3, 0))
    z_dev = (place(1, 0, 0), place(3, 0, 0))
    y_dev = (place(0, 0, 1), place(0, 0, 3))
    y_far = place(0, 0, 2)
    peer = ((z * 4 + x) * 2 + 1 - core, grp)
    partners = x_dev + z_dev + y_dev + (y_far, peer)

    barrier = pltpu.get_barrier_semaphore()
    for other in partners:
        pl.semaphore_signal(barrier, inc=1, device_id=other, device_id_type=pl.DeviceIdType.MESH)

    temper = scale_ref[0]
    offset = bias_ref[0]
    sources = ((img_hbm, img_ref, img, norm_img), (txt_hbm, txt_ref, txt, norm_txt))

    def load(part):
        for hbm, ref, _, _ in sources:
            for half in (0, 1):
                at = rows_at(half * HALF + part * PIECE, PIECE)
                pltpu.make_async_copy(hbm.at[at], ref.at[at], load_sem.at[part]).start()

    def loaded(part):
        pltpu.make_async_copy(img_hbm, img_ref, load_sem.at[part]).wait()

    load(0)
    small = [
        pltpu.make_async_copy(source, target, load_sem.at[2 + at])
        for at, (source, target) in enumerate(((pos_hbm, pos_ref), (cnt_hbm, cnt_ref), (row_hbm, row_ref)))
    ]
    for each in small:
        each.start()

    def normalize(part):
        for _, ref, unit, norm in sources:
            for half in (0, 1):
                at = rows_at(half * HALF + part * PIECE, PIECE)
                values = ref[at, :]
                length = jnp.sqrt(jnp.sum(values * values, axis=1, keepdims=True) + 1e-06)
                norm[at, :] = length
                unit[at, :] = values / length

    loaded(0)
    load(1)
    normalize(0)
    pl.semaphore_wait(barrier, len(partners))

    groups = {}

    def push(group, source, target, device, send):
        at = groups.setdefault(group, len(groups))
        pltpu.make_async_remote_copy(
            src_ref=source, dst_ref=target, send_sem=send_sem.at[send], recv_sem=recv_sem.at[at],
            device_id=device, device_id_type=pl.DeviceIdType.MESH,
        ).start()

    def done(sem, region):
        pltpu.make_async_copy(region, region, sem).wait()

    def arrived(group, region):
        done(recv_sem.at[groups[group]], region)

    rings = {"x": (img, 2 * ROWS, x_dev), "z": (txt, ROWS, z_dev)}

    def place_of(axis, step, side, part):
        stride = rings[axis][1]
        if step == 3:
            return 3 * stride + part * (stride // 2) + side * PIECE
        return stride * step + side * HALF + part * PIECE

    def gather(axis, step, side, part):
        buffer, stride, devices = rings[axis]
        first = {1: side * HALF, 2: (1 - side) * HALF, 3: stride + side * HALF}[step]
        push(
            {1: (axis, 1, side), 2: (axis, 2), 3: (axis, 3, part)}[step],
            buffer.at[rows_at(first + part * PIECE, PIECE)],
            buffer.at[rows_at(place_of(axis, step, side, part), PIECE)],
            devices[side],
            GATHER,
        )

    def near(axis, side):
        buffer, stride, _ = rings[axis]
        arrived((axis, 1, side), buffer.at[rows_at(stride + side * HALF, HALF)])

    def near_rest(axis):
        buffer, stride, _ = rings[axis]
        arrived((axis, 2), buffer.at[rows_at(2 * stride, ROWS)])

    def far(axis, part):
        buffer, stride, _ = rings[axis]
        arrived((axis, 3, part), buffer.at[rows_at(3 * stride + part * (stride // 2), HALF)])

    y_rings = {"yt": (txt, y_txt), "yi": (img, y_img)}

    def gather_y(axis, step, side):
        own, others = y_rings[axis]
        half = side if step != 2 else 1 - side
        if step == 3:
            source = others.at[rows_at(side * ROWS + side * HALF, HALF)]
            target = others.at[rows_at(2 * ROWS + side * HALF, HALF)]
        else:
            source = own.at[rows_at(half * HALF, HALF)]
            target = others.at[rows_at(side * ROWS + half * HALF, HALF)]
        push((axis, 1, side) if step == 1 else (axis, 2), source, target, y_dev[side], ALONG_Y)

    def forward_y(axis):
        others = y_rings[axis][1]
        for side in (0, 1):
            arrived((axis, 1, side), others.at[rows_at(side * ROWS + side * HALF, HALF)])
            gather_y(axis, 3, side)

    def across(step):
        first = 2 * ROWS * step
        push(("c", step), img.at[rows_at(first, ROWS)], img.at[rows_at(first + ROWS, ROWS)], peer, CORE)

    def crossed(step):
        arrived(("c", step), img.at[rows_at(2 * ROWS * step + ROWS, ROWS)])

    def across_far(part):
        first = 6 * ROWS + part * ROWS
        push(("c", 3, part), img.at[rows_at(first, HALF)], img.at[rows_at(first + HALF, HALF)], peer, CORE)

    def crossed_far(part):
        arrived(("c", 3, part), img.at[rows_at(6 * ROWS + part * ROWS + HALF, HALF)])

    def split_rows(source, high, low, first, count):
        for at in range(first, first + count, HALF):
            high[at:at + HALF, :], low[at:at + HALF, :] = split(source[at:at + HALF, :])

    def split_img(first, count=ROWS):
        split_rows(img, img_hi, img_lo, first, count)

    def split_txt(step, first=0, count=ROWS):
        for at in range(ROWS * step + first, ROWS * step + first + count, HALF):
            high, low = split(txt[at:at + HALF, :])
            txt_hi[at:at + HALF, :] = high
            txt_lo[at:at + HALF, :] = low
            both = at + ROWS * step
            txt_both[both:both + HALF, :] = high
            txt_both[both + ROWS:both + ROWS + HALF, :] = low

    def sigmoids(row, rows, col, cols):
        def one(at, count):
            a_hi, a_lo = img_hi[rows_at(at, count), :], img_lo[rows_at(at, count), :]
            wide = cols - cols % 256
            if wide:
                b_hi, b_lo = txt_hi[col:col + wide, :], txt_lo[col:col + wide, :]
                dots = dot_nt(a_hi, b_hi) + (dot_nt(a_hi, b_lo) + dot_nt(a_lo, b_hi))
                sig[rows_at(at, count), col:col + wide] = jax.nn.sigmoid(temper * dots + offset)
            if cols % 256:
                last = col + wide
                both = dot_nt(a_hi, txt_both[2 * last:2 * last + 2 * ROWS, :])
                dots = both[:, :ROWS] + (both[:, ROWS:] + dot_nt(a_lo, txt_hi[last:last + ROWS, :]))
                sig[rows_at(at, count), last:last + ROWS] = jax.nn.sigmoid(temper * dots + offset)

        if rows <= 256:
            one(row, rows)
        else:
            def turn(i, carry):
                one(pl.multiple_of(row + i * 256, 256), 256)
                return carry

            lax.fori_loop(0, rows // 256, turn, 0)

    def times(left, high, low, store):
        l_hi, l_lo = split(left)
        for at, count in COLS:
            cs = slice(at, at + count)
            store(cs, dot_nn(l_hi, high[:, cs]) + (dot_nn(l_hi, low[:, cs]) + dot_nn(l_lo, high[:, cs])))

    def image_grads(first, cols=4 * ROWS):
        def store(cs, value):
            g_img[first:first + 2 * ROWS, cs] = value

        times(sig[first:first + 2 * ROWS, 0:cols], txt_hi.at[0:cols], txt_lo.at[0:cols], store)

    def add_image_grads(first, step, rows=ROWS):
        s_hi, s_lo = split(sig[first:first + rows, ROWS * step:ROWS * (step + 1)])
        s_hi = jnp.concatenate([s_hi, s_hi], axis=1)
        for at, count in COLS:
            cs = slice(at, at + count)
            g_img[first:first + rows, cs] += (
                dot_nn(s_hi, txt_both[2 * ROWS * step:2 * ROWS * (step + 1), cs])
                + dot_nn(s_lo, txt_hi[ROWS * step:ROWS * (step + 1), cs])
            )

    def text_grads(first, row=0, rows=8 * ROWS, add=False):
        def store(cs, value):
            g_txt[first:first + ROWS, cs] = g_txt[first:first + ROWS, cs] + value if add else value

        times(sig[row:row + rows, first:first + ROWS].T, img_hi.at[row:row + rows], img_lo.at[row:row + rows], store)

    def add_text_grads(first, row):
        s_hi, s_lo = split(sig[row:row + ROWS, first:first + ROWS].T)
        s_hi = jnp.concatenate([s_hi, s_hi], axis=1)
        for at, count in COLS:
            cs = slice(at, at + count)
            both = jnp.concatenate([img_hi[row:row + ROWS, cs], img_lo[row:row + ROWS, cs]], axis=0)
            g_txt[first:first + ROWS, cs] += dot_nn(s_hi, both) + dot_nn(s_lo, img_hi[row:row + ROWS, cs])

    for axis in ("x", "z"):
        for side in (0, 1):
            gather(axis, 1, side, 0)
    loaded(1)
    normalize(1)
    for axis in ("x", "z"):
        for side in (0, 1):
            gather(axis, 1, side, 1)
    for part in (0, 1):
        for axis in ("x", "z"):
            for side in (0, 1):
                gather(axis, 2, side, part)
    across(0)
    for each in small:
        each.wait()
    meta[0, 0:4, :] = pos_ref[...]
    meta[0, 4:5, :] = cnt_ref[...]
    meta[0, 5:6, :] = row_ref[...]
    meta[0, 6:8, :] = jnp.zeros((2, ROWS), jnp.int32)
    for slot, device in ((1, y_dev[0]), (2, y_dev[1]), (3, y_far)):
        push("m", meta.at[0], meta.at[slot], device, LISTS)
    for step in (1, 2):
        for side in (0, 1):
            gather_y("yt", step, side)

    split_img(0)
    split_txt(0)
    crossed(0)
    split_img(ROWS)
    sigmoids(0, 256, 0, ROWS)

    arrived("m", meta.at[1:4])
    group_base = blk * (4 * ROWS)
    places = [lax.rem(grp + shift, 4) * ROWS + group_base for shift in (0, 3, 1, 2)]
    tall = lax.broadcasted_iota(jnp.int32, (ROWS, ROWS), 0)

    def named(slot):
        tiles = []
        for ids in range(4):
            hit = None
            for k in range(4):
                listed = jnp.where(meta[slot, 4:5, :] > k, meta[slot, k:k + 1, :], -1)
                same = listed == tall + places[ids]
                hit = same if hit is None else hit | same
            tiles.append(jnp.where(hit, 1.0, 0.0).astype(BF16))
        return jnp.concatenate(tiles, axis=0)

    def held(slot):
        tiles = [
            jnp.where(meta[ids, 5:6, :] == tall + places[slot], 1.0, 0.0).astype(BF16)
            for ids in range(4)
        ]
        return jnp.concatenate(tiles, axis=1)

    own_ids, own_held = named(0), held(0)
    mark_a[:, 0:ROWS] = dot_nn(own_held, own_ids)
    for slot in (1, 2, 3):
        mark_a[:, slot * ROWS:(slot + 1) * ROWS] = dot_nn(own_held, named(slot))
        mark_b[(slot - 1) * ROWS:slot * ROWS, :] = dot_nn(held(slot), own_ids)

    for axis in ("x", "z"):
        for side in (0, 1):
            near(axis, side)
            for part in (0, 1):
                gather(axis, 3, side, part)
        if axis == "x":
            across(1)
    forward_y("yt")
    for step in (1, 2):
        for side in (0, 1):
            gather_y("yi", step, side)

    split_txt(1)
    split_img(256)
    sigmoids(0, 256, ROWS, ROWS)
    sigmoids(256, ROWS, 0, 256)
    crossed(1)
    split_img(256 + ROWS)
    sigmoids(256 + ROWS, ROWS, 0, 256)
    image_grads(256, 2 * ROWS)
    text_grads(ROWS, 0, 512)

    near_rest("x")
    across(2)
    near_rest("z")
    split_txt(2)
    split_img(512)
    sigmoids(0, 512, 2 * ROWS, ROWS)
    add_image_grads(256, 2, 2 * ROWS)
    sigmoids(512, ROWS, 0, 3 * ROWS)
    add_text_grads(ROWS, 512)
    crossed(2)
    split_img(512 + ROWS)
    sigmoids(512 + ROWS, ROWS, 0, 3 * ROWS)
    add_text_grads(ROWS, 512 + ROWS)

    far("x", 0)
    across_far(0)
    far("z", 0)
    split_txt(3, 0, HALF)
    split_img(768, HALF)
    far("x", 1)
    across_far(1)
    far("z", 1)

    def share(step):
        first = 2 * ROWS * step
        push(("r", step), g_img.at[rows_at(first + ROWS, ROWS)], c_in.at[step], peer, CORE)

    def joined(step):
        first = 2 * ROWS * step
        arrived(("r", step), c_in.at[step])
        g_img[first:first + ROWS, :] += c_in[step]

    def share_far(part):
        first = 6 * ROWS + part * ROWS + HALF
        push(("r", 3), g_img.at[rows_at(first, HALF)], c_in.at[3, rows_at(part * HALF, HALF)], peer, CORE)

    def joined_far():
        arrived(("r", 3), c_in.at[3])
        for part in (0, 1):
            first = 6 * ROWS + part * ROWS
            g_img[first:first + HALF, :] += c_in[3, part * HALF:(part + 1) * HALF]

    scatters = {"x": (g_img, 2 * ROWS, x_dev, x_in, x_far), "z": (g_txt, ROWS, z_dev, z_in, z_far)}

    def scatter_near(axis):
        buffer, stride, devices, inbox, _ = scatters[axis]
        for side in (0, 1):
            first = stride + (1 - side) * HALF
            push((axis, "s", 1), buffer.at[rows_at(first, HALF)], inbox.at[0, side], devices[side], SCATTER)

    def scatter_far(axis):
        buffer, stride, devices, _, inbox = scatters[axis]
        for part in (0, 1):
            for side in (0, 1):
                first = place_of(axis, 3, side, part)
                push((axis, "s", 3, part), buffer.at[rows_at(first, PIECE)], inbox.at[part, side], devices[side], SCATTER)

    def scatter_rest(axis, part):
        buffer, stride, devices, inbox, relay = scatters[axis]
        arrived((axis, "s", 3, part), relay.at[part])
        for side in (0, 1):
            first = 2 * stride + (1 - side) * HALF + part * PIECE
            buffer[first:first + PIECE, :] += relay[part, side]
            push(
                (axis, "s", 2, part), buffer.at[rows_at(first, PIECE)], inbox.at[1 + part, side, rows_at(0, PIECE)],
                devices[side], SCATTER,
            )

    split_txt(3, HALF, HALF)
    sigmoids(256, 256, 3 * ROWS, ROWS)
    add_image_grads(256 + ROWS, 3)
    share(1)
    add_image_grads(256, 3)

    @pl.when(core == 0)
    def _():
        joined(1)
        scatter_near("x")

    split_img(896, HALF)
    crossed_far(0)
    split_img(768 + HALF, HALF)
    sigmoids(768, ROWS, ROWS, ROWS)
    add_text_grads(ROWS, 768)
    crossed_far(1)
    split_img(896 + HALF, HALF)
    sigmoids(896, ROWS, ROWS, ROWS)
    add_text_grads(ROWS, 896)
    scatter_near("z")
    @pl.when(core == 1)
    def _():
        joined(1)
        scatter_near("x")

    sigmoids(768, 256, 0, ROWS)
    sigmoids(768, 256, 2 * ROWS, 2 * ROWS)
    image_grads(768)
    share_far(0)
    share_far(1)
    sigmoids(0, 256, 3 * ROWS, ROWS)
    sigmoids(512, 256, 3 * ROWS, ROWS)
    text_grads(3 * ROWS)
    scatter_far("z")
    joined_far()
    scatter_far("x")

    forward_y("yi")

    image_grads(512)
    share(2)
    text_grads(2 * ROWS)
    sig[0:ROWS, 0:ROWS] -= mark_a[:, 0:ROWS]
    image_grads(0)
    share(0)
    text_grads(0)
    joined(2)
    scatter_rest("x", 0)
    scatter_rest("z", 0)

    arrived(("yt", 2), y_txt.at[ROWS:3 * ROWS])
    split_rows(y_txt, yt_hi, yt_lo, 0, 3 * ROWS)
    own = rows_at(0, ROWS)
    dots = dot_nt(img_hi[own, :], yt_hi[...]) + (dot_nt(img_hi[own, :], yt_lo[...]) + dot_nt(img_lo[own, :], yt_hi[...]))
    coef = mark_a[:, ROWS:4 * ROWS] * (jax.nn.sigmoid(temper * dots + offset) - 1.0)

    def add_img(cs, value):
        g_img[0:ROWS, cs] += value

    times(coef, yt_hi, yt_lo, add_img)
    scatter_rest("x", 1)
    scatter_rest("z", 1)
    joined(0)

    arrived(("yi", 2), y_img.at[ROWS:3 * ROWS])
    split_rows(y_img, yi_hi, yi_lo, 0, 3 * ROWS)
    dots = dot_nt(yi_hi[...], txt_hi[own, :]) + (dot_nt(yi_hi[...], txt_lo[own, :]) + dot_nt(yi_lo[...], txt_hi[own, :]))
    coef = mark_b[...] * (jax.nn.sigmoid(temper * dots + offset) - 1.0)

    def add_txt(cs, value):
        g_txt[0:ROWS, cs] += value

    times(coef.T, yi_hi, yi_lo, add_txt)

    ends = (
        ("x", g_img, x_in, img, norm_img, gimg_ref),
        ("z", g_txt, z_in, txt, norm_txt, gtxt_ref),
    )
    for axis, sums, inbox, unit, norm, out in ends:
        arrived((axis, "s", 1), inbox.at[0])
        for side in (0, 1):
            at = slice((1 - side) * HALF, (2 - side) * HALF)
            sums[at, :] += inbox[0, side]
    for part in (0, 1):
        for axis, sums, inbox, unit, norm, out in ends:
            arrived((axis, "s", 2, part), inbox.at[1 + part, :, rows_at(0, PIECE)])
            for half in (0, 1):
                at = slice(half * HALF + part * PIECE, half * HALF + (part + 1) * PIECE)
                grad = temper * (sums[at, :] + inbox[1 + part, half, 0:PIECE])
                units = unit[at, :]
                along = jnp.sum(units * grad, axis=1, keepdims=True)
                out[at, :] = (grad - units * along) / norm[at, :]

    done(send_sem.at[CORE], g_img)
    done(send_sem.at[GATHER], g_img.at[0:6 * ROWS])
    done(send_sem.at[ALONG_Y], g_img.at[0:6 * ROWS])
    done(send_sem.at[SCATTER], g_img.at[0:6 * ROWS])
    done(send_sem.at[LISTS], meta.at[1:4])


def hand_on(gimg_in, gtxt_in, gimg_out, gtxt_out, sems):
    copies = [
        pltpu.make_async_copy(gimg_in, gimg_out, sems.at[0]),
        pltpu.make_async_copy(gtxt_in, gtxt_out, sems.at[1]),
    ]
    for copy in copies:
        copy.start()
    for copy in copies:
        copy.wait()


def body(image_emb, text_emb, logit_scale, logit_bias, pos_image, pos_count, image_row):
    anywhere = pl.BlockSpec(memory_space=pl.ANY)
    vmem = pl.BlockSpec(memory_space=pltpu.VMEM)
    rows = jax.ShapeDtypeStruct((ROWS, D), F32)
    grads = pl.pallas_call(
        kernel,
        out_shape=(pltpu.VMEM((ROWS, D), F32), pltpu.VMEM((ROWS, D), F32)),
        in_specs=[pl.BlockSpec(memory_space=pltpu.SMEM)] * 2 + [pl.BlockSpec(memory_space=pltpu.HBM)] * 5,
        out_specs=(vmem, vmem),
        scratch_shapes=[
            pltpu.VMEM((ROWS, D), F32),
            pltpu.VMEM((ROWS, D), F32),
            pltpu.VMEM((4, ROWS), jnp.int32),
            pltpu.VMEM((1, ROWS), jnp.int32),
            pltpu.VMEM((1, ROWS), jnp.int32),
            pltpu.SemaphoreType.DMA((5,)),
            pltpu.VMEM((8 * ROWS, D), F32),
            pltpu.VMEM((4 * ROWS, D), F32),
            pltpu.VMEM((8 * ROWS, D), BF16),
            pltpu.VMEM((8 * ROWS, D), BF16),
            pltpu.VMEM((4 * ROWS, D), BF16),
            pltpu.VMEM((4 * ROWS, D), BF16),
            pltpu.VMEM((8 * ROWS, 4 * ROWS), F32),
            pltpu.VMEM((8 * ROWS, D), F32),
            pltpu.VMEM((4 * ROWS, D), F32),
            pltpu.VMEM((3 * ROWS, D), F32),
            pltpu.VMEM((3 * ROWS, D), F32),
            pltpu.VMEM((3 * ROWS, D), BF16),
            pltpu.VMEM((3 * ROWS, D), BF16),
            pltpu.VMEM((3 * ROWS, D), BF16),
            pltpu.VMEM((3 * ROWS, D), BF16),
            pltpu.VMEM((8 * ROWS, D), BF16),
            pltpu.VMEM((3, 2, HALF, D), F32),
            pltpu.VMEM((3, 2, HALF, D), F32),
            pltpu.VMEM((2, 2, PIECE, D), F32),
            pltpu.VMEM((2, 2, PIECE, D), F32),
            pltpu.VMEM((4, ROWS, D), F32),
            pltpu.VMEM((4, 8, ROWS), jnp.int32),
            pltpu.VMEM((ROWS, 4 * ROWS), F32),
            pltpu.VMEM((3 * ROWS, ROWS), F32),
            pltpu.VMEM((ROWS, 1), F32),
            pltpu.VMEM((ROWS, 1), F32),
            pltpu.SemaphoreType.DMA((N_SEND,)),
            pltpu.SemaphoreType.DMA((N_RECV,)),
        ],
        compiler_params=pltpu.CompilerParams(
            collective_id=0, has_side_effects=True, vmem_limit_bytes=46 * 2**20
        ),
        name="align_step",
    )(
        logit_scale,
        logit_bias,
        *(
            pltpu.with_memory_space_constraint(operand, pltpu.HBM)
            for operand in (
                image_emb, text_emb, pos_image.T, pos_count.reshape(1, ROWS), image_row.reshape(1, ROWS),
            )
        ),
    )
    grads = [pltpu.with_memory_space_constraint(grad, pltpu.VMEM) for grad in grads]
    return pl.pallas_call(
        hand_on,
        out_shape=(rows, rows),
        in_specs=[anywhere, anywhere],
        out_specs=(anywhere, anywhere),
        scratch_shapes=[pltpu.SemaphoreType.DMA((2,))],
        name="hand_on",
    )(*grads)


def solution(mesh):
    return jax.shard_map(
        body,
        mesh=mesh,
        in_specs=(
            P(("blk", "grp"), None),
            P(("blk", "grp"), None),
            P(),
            P(),
            P(("blk", "grp"), None),
            P(("blk", "grp")),
            P(("blk", "grp")),
        ),
        out_specs=(P(("blk", "grp"), None), P(("blk", "grp"), None)),
        check_vma=False,
    )
```
